128 devices in a mesh: row: 8 (over z, x_lo), col: 16 (over x_hi, y, core).
Axes of the slice: x: 4 (x_hi: 2, x_lo: 2; x = x_hi * 2 + x_lo), y: 4, z: 4, core: 2. Of those that a mesh axis runs over, the one named last changes fastest.
Arguments:
- frames: bfloat16 [2, 1024, 1024, 128], P(None, 'row', 'col'), may hold values from -6 to 6
- conv_weight: bfloat16 [3, 3, 128, 128], replicated, may hold values from -0.1875 to 0.1875
- embed_weight: bfloat16 [32768, 2048], P('row', 'col'), may hold values from -0.03125 to 0.03125
- unembed_weight: bfloat16 [32768, 2048], P('row', 'col'), may hold values from -0.125 to 0.125
- qkv_weight: bfloat16 [3, 2048, 2048], P(None, None, 'col'), may hold values from -0.261584 to 0.261584
- out_weight: bfloat16 [2048, 2048], P('col'), may hold values from -0.125 to 0.125
Outputs:
- denoised: bfloat16 [2, 1024, 1024, 128], P(None, 'row', 'col')
The draws below stay inside these ranges and needn't reach their ends.
All inputs are finite; a program needn't handle non-finite values.
Results may differ from the reference program's by a relative error of at most 0.025.
Values may be sent and summed in bfloat16 or wider, within the bound.
No kernel may reach another device: no remote copies, remote signals or barrier semaphores. Data moves between devices by JAX's collectives and lax.ppermute only.
A program may use at most 128 MiB of HBM per device.

```python
import jax
import jax.numpy as jnp
from jax import lax

C = 128
D = 2048
HEADS = 16
HEAD = 128
POOL = 4
PATCH = 16
PROWS = 2
FRAMES = 2
H = 1024
W = 1024
PIX = 32768
TOKENS = 512
N_ROW = 8
N_COL = 16


def draw_qkv_weight(key, part):
    key = jax.random.fold_in(key, 7)
    base_key = jax.random.fold_in(key, 0)
    weight = jnp.clip(jax.random.normal(base_key, (3, D, D), jnp.float32), -5.0, 5.0) * D ** (-0.5)
    return weight.astype(jnp.bfloat16)


def steps_of(own_key, dims, pieces, low, largest):
    level, own = 1.0, jax.random.fold_in(own_key, 6)
    for dim, shards_of in pieces:
        draws = jnp.exp(jax.random.uniform(jax.random.fold_in(own, dim), (shards_of,), jnp.float32, low / len(pieces), largest / len(pieces)))
        level = level * jnp.repeat(draws, dims[dim] // shards_of).reshape([-1 if axis == dim else 1 for axis in range(len(dims))])
    return level


def noise(stream_key, extent, scale, most, pieces=(), dtype=jnp.bfloat16):
    values = jax.random.normal(stream_key, extent, jnp.float32) * scale
    if len(pieces) > 0:
        values = steps_of(stream_key, extent, pieces, -0.22, 0.18) * values
    return jnp.clip(values, min=-most, max=most).astype(dtype)


def setup_inputs(seed: int = 0) -> dict:
    arg_keys = jax.random.split(jax.random.key(seed), 7)
    frames = noise(arg_keys[0], (FRAMES, H, W, C), 1.0, 6.0, ((1, 8), (2, 16)))
    conv_weight = noise(arg_keys[1], (3, 3, C, C), (9 * C) ** -0.5, 0.1875)
    embed_weight = noise(arg_keys[2], (PIX, D), PIX ** -0.5, 0.03125, ((0, 8), (1, 16)))
    unembed_weight = noise(arg_keys[3], (PIX, D), D ** -0.5, 0.125, ((0, 8), (1, 16)))
    qkv_weight = draw_qkv_weight(jax.random.fold_in(arg_keys[6], 71), 0)
    out_weight = noise(arg_keys[5], (D, D), D ** -0.5, 0.125, ((0, 16),))
    return dict(frames=frames, conv_weight=conv_weight, embed_weight=embed_weight, unembed_weight=unembed_weight, qkv_weight=qkv_weight, out_weight=out_weight)


def convolve(frame, conv_weight):
    height, width, channels = frame.shape
    padded = jnp.pad(frame, ((1, 1), (1, 1), (0, 0)))
    total = jnp.zeros((height * width, channels), jnp.float32)
    for row_shift in range(3):
        for col_shift in range(3):
            window = padded[row_shift:row_shift + height, col_shift:col_shift + width, :].reshape(height * width, channels)
            total = total + jnp.dot(window, conv_weight[row_shift, col_shift], preferred_element_type=jnp.float32)
    return total.reshape(height, width, channels)

def residual_block(frame, conv_weight):
    convolved = convolve(frame, conv_weight)
    scaled = convolved * lax.rsqrt(lax.optimization_barrier(jnp.mean(convolved * convolved, axis=-1, keepdims=True)) + 1e-06)
    return frame.astype(jnp.float32) + jax.nn.silu(scaled)

def attend_head(inputs):
    query_head, key_head, value_head = inputs
    scores = jnp.dot(query_head, key_head.T, preferred_element_type=jnp.float32) * HEAD ** (-0.5)
    weights = jax.nn.softmax(scores, axis=-1).astype(jnp.bfloat16)
    return jnp.dot(weights, value_head, preferred_element_type=jnp.float32).astype(jnp.bfloat16)

def reference(frames, conv_weight, embed_weight, unembed_weight, qkv_weight, out_weight):
    features = lax.map(lambda frame: residual_block(frame, conv_weight), frames)
    pooled = features.reshape(FRAMES, H // POOL, POOL, W // POOL, POOL, C).mean(axis=(2, 4)).astype(jnp.bfloat16)
    patches = pooled.reshape(FRAMES, N_ROW, PROWS, PATCH, N_COL, PATCH, C).transpose(1, 4, 0, 2, 3, 5, 6).reshape(TOKENS, PIX)
    embedded = jnp.dot(patches, embed_weight, preferred_element_type=jnp.float32).astype(jnp.bfloat16)
    wide = embedded.astype(jnp.float32)
    normed = (wide * lax.rsqrt(lax.optimization_barrier(jnp.mean(wide * wide, axis=-1, keepdims=True)) + 1e-06)).astype(jnp.bfloat16)
    queries = jnp.dot(normed, qkv_weight[0], preferred_element_type=jnp.float32).astype(jnp.bfloat16)
    keys = jnp.dot(normed, qkv_weight[1], preferred_element_type=jnp.float32).astype(jnp.bfloat16)
    values = jnp.dot(normed, qkv_weight[2], preferred_element_type=jnp.float32).astype(jnp.bfloat16)

    def by_head(array):
        return array.reshape(TOKENS, HEADS, HEAD).transpose(1, 0, 2)
    attended = lax.map(attend_head, (by_head(queries), by_head(keys), by_head(values)))
    attended = attended.transpose(1, 0, 2).reshape(TOKENS, D)
    projected = jnp.dot(attended, out_weight, preferred_element_type=jnp.float32)
    mixed = (embedded.astype(jnp.float32) + projected).astype(jnp.bfloat16)
    patch_values = lax.dot_general(mixed, unembed_weight, (((1,), (1,)), ((), ())), preferred_element_type=jnp.float32).astype(jnp.bfloat16)
    small_image = patch_values.reshape(N_ROW, N_COL, FRAMES, PROWS, PATCH, PATCH, C).transpose(2, 0, 3, 4, 1, 5, 6).reshape(FRAMES, H // POOL, W // POOL, C)

    def finish(pair):
        frame_features, frame_small = pair
        upsampled = jnp.repeat(jnp.repeat(frame_small, POOL, axis=0), POOL, axis=1)
        return (frame_features + upsampled.astype(jnp.float32)).astype(jnp.bfloat16)
    return lax.map(finish, (features, small_image))
```

```python
import functools

import jax
import jax.numpy as jnp
from jax import lax
from jax.experimental import pallas as pl
from jax.experimental.pallas import tpu as pltpu
from jax.sharding import PartitionSpec as P

C = 128
BF = jnp.bfloat16
F32 = jnp.float32
EPS = 1e-06
ROW = ("z", "xl")
COL = ("xh", "y", "core")
ROWY = ROW + ("y",)
EVERY = ROW + COL
CHUNK = 32
SUB = 16
LEFT = 8


def params(mib=56):
    return pltpu.CompilerParams(vmem_limit_bytes=mib * 2**20)


def whole(shape):
    return pl.BlockSpec(shape, lambda *_: (0,) * len(shape))


def conv_kernel(
    main, above, below, top, bottom, left, right, weight, features, send, padded, taps, kernel, pooled
):
    frame, step = pl.program_id(0), pl.program_id(1)
    steps = pl.num_programs(1)

    @pl.when((frame == 0) & (step == 0))
    def _():
        for a in range(3):
            for k in range(4):
                for o in range(2):
                    b = k - o
                    block = weight[a, b] if 0 <= b <= 2 else jnp.zeros((C, C), BF)
                    kernel[pl.ds(a * 512 + k * C, C), pl.ds(o * C, C)] = block

    cols = pl.ds(LEFT, 64)
    padded[pl.ds(1, CHUNK), cols, :] = main[0].astype(F32)
    first = jnp.where(step == 0, top[0, 0].astype(F32), above[0, 0].astype(F32))
    padded[0, cols, :] = first
    last = jnp.where(step == steps - 1, bottom[0, 0].astype(F32), below[0, 0].astype(F32))
    padded[CHUNK + 1, cols, :] = last
    rows = pl.ds(pl.multiple_of(step * CHUNK, CHUNK), CHUNK + 2)
    padded[:, LEFT - 1, :] = left[0, rows, :]
    padded[:, LEFT + 64, :] = right[0, rows, :]
    for k in range(6):
        taps[:, :, pl.ds(k * C, C)] = padded[:, pl.ds(LEFT - 1 + k, 16, stride=4), :].astype(BF)

    for sub in range(CHUNK // SUB):
        total = [jnp.zeros((SUB // 4, 16, C), F32)]
        for pair in range(2):
            lhs = jnp.concatenate(
                [
                    taps[pl.ds(sub * SUB + a, SUB), :, pl.ds(pair * 256, 512)].reshape(SUB * 16, 512)
                    for a in range(3)
                ],
                axis=1,
            )
            result = jnp.dot(lhs, kernel[...], preferred_element_type=F32)
            for o in range(2):
                m = pair * 2 + o
                v = result[:, o * C : (o + 1) * C]
                mean = jnp.mean(v * v, axis=-1, keepdims=True)
                s = v * lax.rsqrt(mean + EPS)
                x = taps[pl.ds(sub * SUB + 1, SUB), :, pl.ds((m + 1) * C, C)].reshape(SUB * 16, C)
                f = x.astype(F32) + s * (0.5 + 0.5 * jnp.tanh(0.5 * s))
                f = f.reshape(SUB, 16, C)
                features[0, pl.ds(sub * SUB, SUB), m] = f.astype(BF)
                total.append(f.reshape(SUB // 4, 4, 16, C).sum(axis=1))
        mean = sum(total) * (1.0 / 16.0)
        for g in range(SUB // 4):
            q = sub * (SUB // 4) + g
            token = frame * 2 + step // 2
            for half in range(2):
                piece = ((step % 2) * 4 + q // 2) * 4 + (q % 2) * 2 + half
                at = pl.ds(pl.multiple_of(token * 8, 8), 8)
                pooled[piece, at, :] = mean[g, half * 8 : half * 8 + 8]

    @pl.when((frame == 1) & (step == steps - 1))
    def _():
        for r in range(8):
            for y in range(4):
                block = pooled[r * 4 + y].astype(BF)
                for xh in range(2):
                    for core in range(2):
                        send[((r * 2 + xh) * 4 + y) * 2 + core] = block


def convolve(frames, top, bottom, left, right, weight):
    steps = 128 // CHUNK
    return pl.pallas_call(
        conv_kernel,
        grid=(2, steps),
        in_specs=[
            pl.BlockSpec((1, CHUNK, 64, C), lambda f, i: (f, i, 0, 0)),
            pl.BlockSpec((1, 1, 64, C), lambda f, i: (f, jnp.maximum(i * CHUNK - 1, 0), 0, 0)),
            pl.BlockSpec((1, 1, 64, C), lambda f, i: (f, jnp.minimum((i + 1) * CHUNK, 127), 0, 0)),
            pl.BlockSpec((1, 1, 64, C), lambda f, i: (f, 0, 0, 0)),
            pl.BlockSpec((1, 1, 64, C), lambda f, i: (f, 0, 0, 0)),
            pl.BlockSpec((1, 130, C), lambda f, i: (f, 0, 0)),
            pl.BlockSpec((1, 130, C), lambda f, i: (f, 0, 0)),
            whole((3, 3, C, C)),
        ],
        out_specs=[
            pl.BlockSpec((1, CHUNK, 4, 16, C), lambda f, i: (f, i, 0, 0, 0)),
            whole((128, 32, C)),
        ],
        out_shape=[
            jax.ShapeDtypeStruct((2, 128, 4, 16, C), BF),
            jax.ShapeDtypeStruct((128, 32, C), BF),
        ],
        scratch_shapes=[
            pltpu.VMEM((CHUNK + 2, 80, C), F32),
            pltpu.VMEM((CHUNK + 2, 16, 6 * C), BF),
            pltpu.VMEM((3 * 512, 2 * C), BF),
            pltpu.VMEM((32, 32, C), F32),
        ],
        compiler_params=params(),
        cost_estimate=pl.CostEstimate(
            flops=2 * 16384 * 9 * C * C, bytes_accessed=9 * 2**20, transcendentals=2 * 16384 * C
        ),
        name="conv_block",
    )(frames, frames, frames, top, bottom, left, right, weight)


def embed_kernel(received, weight, out, rows, values, wide):
    rows[...] = received[...].reshape(4096, C).astype(F32)
    for j in range(8):
        values[:, pl.ds(j * C, C)] = rows[pl.ds(j, 512, stride=8), :].astype(BF)
    for y in range(4):
        wide[:, pl.ds(y * C, C)] = weight[y]
    for half in range(2):
        result = jnp.dot(
            values[pl.ds(half * 256, 256), :], wide[...], preferred_element_type=F32
        ).astype(BF)
        for r in range(4):
            for y in range(4):
                out[(half * 4 + r) * 4 + y] = result[r * 64 : r * 64 + 64, y * C : y * C + C]


def embed(received, weight):
    return pl.pallas_call(
        embed_kernel,
        out_shape=jax.ShapeDtypeStruct((32, 64, C), BF),
        scratch_shapes=[
            pltpu.VMEM((4096, C), F32),
            pltpu.VMEM((512, 1024), BF),
            pltpu.VMEM((1024, 512), BF),
        ],
        compiler_params=params(),
        name="embed",
    )(received, weight)


def sum_kernel(copies, terms, *rest):
    out, total_out = rest[-2:]
    total = terms[0].astype(F32)
    for i in range(1, terms.shape[0]):
        total = total + terms[i].astype(F32)
    if len(rest) == 3:
        total = rest[0][...].astype(F32) + total
    total = total.astype(BF)
    total_out[...] = total
    for i in range(copies):
        out[i] = total


def sum_and_copy(copies, terms, *base):
    return pl.pallas_call(
        functools.partial(sum_kernel, copies),
        out_shape=[
            jax.ShapeDtypeStruct((copies, 64, C), BF),
            jax.ShapeDtypeStruct((64, C), BF),
        ],
        compiler_params=params(),
        name="sum_and_copy",
    )(terms, *base)


def qkv_kernel(embedded, weight, queries, pairs):
    square = jnp.zeros((64, 1), F32)
    for c in range(16):
        block = embedded[c].astype(F32)
        square = square + jnp.sum(block * block, axis=-1, keepdims=True)
    scale = lax.rsqrt(square * (1.0 / 2048.0) + EPS)
    normed = jnp.concatenate(
        [(embedded[c].astype(F32) * scale).astype(BF) for c in range(16)], axis=1
    )
    queries[...] = jnp.dot(normed, weight[0], preferred_element_type=F32).astype(BF)
    for part in range(2):
        result = jnp.dot(normed, weight[1 + part], preferred_element_type=F32).astype(BF)
        for r in range(8):
            pairs[r, part] = result


def project_qkv(embedded, weight):
    return pl.pallas_call(
        qkv_kernel,
        out_shape=[
            jax.ShapeDtypeStruct((64, C), BF),
            jax.ShapeDtypeStruct((8, 2, 64, C), BF),
        ],
        compiler_params=params(),
        name="qkv",
    )(embedded, weight)


def attend_kernel(queries, pairs, weight, out):
    keys = pairs[:, 0].reshape(512, C)
    values = pairs[:, 1].reshape(512, C)
    scores = lax.dot_general(
        queries[...], keys, (((1,), (1,)), ((), ())), preferred_element_type=F32
    ) * C ** (-0.5)
    scores = jnp.exp(scores - jnp.max(scores, axis=-1, keepdims=True))
    weights = (scores / jnp.sum(scores, axis=-1, keepdims=True)).astype(BF)
    attended = jnp.dot(weights, values, preferred_element_type=F32).astype(BF)
    projected = jnp.dot(attended, weight[...], preferred_element_type=F32).astype(BF)
    for c in range(16):
        out[c] = projected[:, c * C : (c + 1) * C]


def attend(queries, pairs, weight):
    return pl.pallas_call(
        attend_kernel,
        out_shape=jax.ShapeDtypeStruct((16, 64, C), BF),
        compiler_params=params(),
        name="attend",
    )(queries, pairs, weight)


def unembed_kernel(mixed, weight, out, values, wide, rows):
    for y in range(4):
        wide[:, pl.ds(y * C, C)] = weight[y]
        for r in range(8):
            values[pl.ds(r * 64, 64), pl.ds(y * C, C)] = mixed[r * 4 + y]
    for j in range(8):
        rows[pl.ds(j, 512, stride=8), :] = lax.dot_general(
            values[...],
            wide[pl.ds(j * C, C), :],
            (((1,), (1,)), ((), ())),
            preferred_element_type=F32,
        )
    out[...] = rows[...].astype(BF).reshape(128, 32, C)


def unembed(mixed, weight):
    return pl.pallas_call(
        unembed_kernel,
        out_shape=jax.ShapeDtypeStruct((128, 32, C), BF),
        scratch_shapes=[
            pltpu.VMEM((512, 512), BF),
            pltpu.VMEM((1024, 512), BF),
            pltpu.VMEM((4096, C), F32),
        ],
        compiler_params=params(),
        name="unembed",
    )(mixed, weight)


def finish_kernel(features, received, out, patch, spread):
    frame, step = pl.program_id(0), pl.program_id(1)

    @pl.when((frame == 0) & (step == 0))
    def _():
        for r in range(8):
            for y in range(4):
                total = jnp.zeros((32, C), F32)
                for xh in range(2):
                    for core in range(2):
                        total = total + received[((r * 2 + xh) * 4 + y) * 2 + core].astype(F32)
                patch[r * 4 + y] = total.astype(BF).astype(F32)

    token = frame * 2 + step // 2
    at = pl.ds(pl.multiple_of(token * 8, 8), 8)
    for q in range(CHUNK // 4):
        piece = ((step % 2) * 4 + q // 2) * 4 + (q % 2) * 2
        small = jnp.concatenate([patch[piece, at, :], patch[piece + 1, at, :]], axis=0)
        for row in range(4):
            for m in range(4):
                value = features[0, q * 4 + row, m].astype(F32) + small
                spread[q * 4 + row, pl.ds(m, 16, stride=4), :] = value
    out[0] = spread[...].astype(BF)


def finish(features, received):
    return pl.pallas_call(
        finish_kernel,
        grid=(2, 128 // CHUNK),
        in_specs=[
            pl.BlockSpec((1, CHUNK, 4, 16, C), lambda f, i: (f, i, 0, 0, 0)),
            whole((128, 32, C)),
        ],
        out_specs=pl.BlockSpec((1, CHUNK, 64, C), lambda f, i: (f, i, 0, 0)),
        out_shape=jax.ShapeDtypeStruct((2, 128, 64, C), BF),
        scratch_shapes=[
            pltpu.VMEM((32, 32, C), F32),
            pltpu.VMEM((CHUNK, 64, C), F32),
        ],
        compiler_params=params(),
        name="finish",
    )(features, received)


def exchange(array, axes):
    return lax.all_to_all(array, axes, 0, 0, tiled=True)


def from_neighbours(low, high, axes, count):
    forward = [(i, i + 1) for i in range(count - 1)]
    backward = [(i + 1, i) for i in range(count - 1)]
    return lax.ppermute(low, axes, forward), lax.ppermute(high, axes, backward)


def on_device(frames, conv_weight, embed_weight, unembed_weight, qkv_weight, out_weight):
    top, bottom = from_neighbours(frames[:, 127:], frames[:, :1], ROW, 8)
    edges = [
        jnp.concatenate([top[:, :, x], frames[:, :, x], bottom[:, :, x]], axis=1) for x in (63, 0)
    ]
    left, right = from_neighbours(edges[0], edges[1], COL, 16)
    embed_part = exchange(embed_weight.reshape(4, 1024, C), "y")
    unembed_part = exchange(unembed_weight.reshape(4, 1024, C), "y")
    features, patches = convolve(
        frames, top, bottom, left.astype(F32), right.astype(F32), conv_weight
    )
    partial = embed(exchange(patches, EVERY), embed_part)
    copies, embedded = sum_and_copy(16, exchange(partial, ROWY))
    queries, pairs = project_qkv(exchange(copies, COL), qkv_weight)
    projected = attend(queries, exchange(pairs, ROW), out_weight)
    copies, _ = sum_and_copy(32, exchange(projected, COL), embedded)
    patch_values = unembed(exchange(copies, ROWY), unembed_part)
    return finish(features, exchange(patch_values, EVERY))


def solution(mesh):
    fine = jax.sharding.Mesh(mesh.devices.reshape(4, 2, 2, 4, 2), EVERY)
    placed = (
        P(None, ROW, COL, None),
        P(),
        P(ROW, COL),
        P(ROW, COL),
        P(None, None, COL),
        P(COL, None),
    )
    return jax.shard_map(
        on_device,
        mesh=fine,
        in_specs=placed,
        out_specs=P(None, ROW, COL, None),
        check_vma=False,
    )
```

```python
import functools

import jax
import jax.numpy as jnp
from jax import lax
from jax.experimental import pallas as pl
from jax.experimental.pallas import tpu as pltpu
from jax.sharding import PartitionSpec as P

C = 128
BF = jnp.bfloat16
F32 = jnp.float32
EPS = 1e-06
ROW = ("z", "xl")
COL = ("xh", "y", "core")
ROWY = ROW + ("y",)
SAME = ROW + ("xh", "y")
EVERY = ROW + COL
CHUNK = 32
SUB = 16
LEFT = 8


def params(mib=56):
    return pltpu.CompilerParams(vmem_limit_bytes=mib * 2**20)


def whole(shape):
    return pl.BlockSpec(shape, lambda *_: (0,) * len(shape))


def conv_kernel(
    main, above, below, top, bottom, left, right, weight, features, send, padded, taps, kernel, pooled
):
    frame, step = pl.program_id(0), pl.program_id(1)
    steps = pl.num_programs(1)

    @pl.when((frame == 0) & (step == 0))
    def _():
        for a in range(3):
            for k in range(4):
                for o in range(2):
                    b = k - o
                    block = weight[a, b] if 0 <= b <= 2 else jnp.zeros((C, C), BF)
                    kernel[pl.ds(a * 512 + k * C, C), pl.ds(o * C, C)] = block

    cols = pl.ds(LEFT, 64)
    padded[pl.ds(1, CHUNK), cols, :] = main[0].astype(F32)
    first = jnp.where(step == 0, top[0, 0].astype(F32), above[0, 0].astype(F32))
    padded[0, cols, :] = first
    last = jnp.where(step == steps - 1, bottom[0, 0].astype(F32), below[0, 0].astype(F32))
    padded[CHUNK + 1, cols, :] = last
    rows = pl.ds(pl.multiple_of(step * CHUNK, CHUNK), CHUNK + 2)
    padded[:, LEFT - 1, :] = left[0, rows, :]
    padded[:, LEFT + 64, :] = right[0, rows, :]
    for k in range(6):
        taps[:, :, pl.ds(k * C, C)] = padded[:, pl.ds(LEFT - 1 + k, 16, stride=4), :].astype(BF)

    for sub in range(CHUNK // SUB):
        total = [jnp.zeros((SUB // 4, 16, C), F32)]
        for pair in range(2):
            lhs = jnp.concatenate(
                [
                    taps[pl.ds(sub * SUB + a, SUB), :, pl.ds(pair * 256, 512)].reshape(SUB * 16, 512)
                    for a in range(3)
                ],
                axis=1,
            )
            result = jnp.dot(lhs, kernel[...], preferred_element_type=F32)
            for o in range(2):
                m = pair * 2 + o
                v = result[:, o * C : (o + 1) * C]
                mean = jnp.mean(v * v, axis=-1, keepdims=True)
                s = v * lax.rsqrt(mean + EPS)
                x = taps[pl.ds(sub * SUB + 1, SUB), :, pl.ds((m + 1) * C, C)].reshape(SUB * 16, C)
                f = x.astype(F32) + s * (0.5 + 0.5 * jnp.tanh(0.5 * s))
                f = f.reshape(SUB, 16, C)
                features[0, pl.ds(sub * SUB, SUB), m] = f.astype(BF)
                total.append(f.reshape(SUB // 4, 4, 16, C).sum(axis=1))
        mean = sum(total) * (1.0 / 16.0)
        for g in range(SUB // 4):
            q = sub * (SUB // 4) + g
            token = frame * 2 + step // 2
            for half in range(2):
                piece = ((step % 2) * 4 + q // 2) * 4 + (q % 2) * 2 + half
                at = pl.ds(pl.multiple_of(token * 8, 8), 8)
                pooled[piece, at, :] = mean[g, half * 8 : half * 8 + 8]

    @pl.when((frame == 1) & (step == steps - 1))
    def _():
        for r in range(8):
            for y in range(4):
                block = pooled[r * 4 + y].astype(BF)
                for xh in range(2):
                    send[(r * 2 + xh) * 4 + y] = block


def convolve(frames, top, bottom, left, right, weight):
    steps = 128 // CHUNK
    return pl.pallas_call(
        conv_kernel,
        grid=(2, steps),
        in_specs=[
            pl.BlockSpec((1, CHUNK, 64, C), lambda f, i: (f, i, 0, 0)),
            pl.BlockSpec((1, 1, 64, C), lambda f, i: (f, jnp.maximum(i * CHUNK - 1, 0), 0, 0)),
            pl.BlockSpec((1, 1, 64, C), lambda f, i: (f, jnp.minimum((i + 1) * CHUNK, 127), 0, 0)),
            pl.BlockSpec((1, 1, 64, C), lambda f, i: (f, 0, 0, 0)),
            pl.BlockSpec((1, 1, 64, C), lambda f, i: (f, 0, 0, 0)),
            pl.BlockSpec((1, 130, C), lambda f, i: (f, 0, 0)),
            pl.BlockSpec((1, 130, C), lambda f, i: (f, 0, 0)),
            whole((3, 3, C, C)),
        ],
        out_specs=[
            pl.BlockSpec((1, CHUNK, 4, 16, C), lambda f, i: (f, i, 0, 0, 0)),
            whole((64, 32, C)),
        ],
        out_shape=[
            jax.ShapeDtypeStruct((2, 128, 4, 16, C), BF),
            jax.ShapeDtypeStruct((64, 32, C), BF),
        ],
        scratch_shapes=[
            pltpu.VMEM((CHUNK + 2, 80, C), F32),
            pltpu.VMEM((CHUNK + 2, 16, 6 * C), BF),
            pltpu.VMEM((3 * 512, 2 * C), BF),
            pltpu.VMEM((32, 32, C), F32),
        ],
        compiler_params=params(),
        cost_estimate=pl.CostEstimate(
            flops=2 * 16384 * 9 * C * C, bytes_accessed=9 * 2**20, transcendentals=2 * 16384 * C
        ),
        name="conv_block",
    )(frames, frames, frames, top, bottom, left, right, weight)


def embed_kernel(received, own, other, later_own, later_other, out, rows, values, wide):
    core = lax.axis_index("core")
    rows[...] = received[...].reshape(2048, C).astype(F32)
    for j in range(8):
        values[:, pl.ds(j * C, C)] = rows[pl.ds(j, 256, stride=8), :].astype(BF)
    for which, weight in enumerate((own, other)):
        for y in range(4):
            wide[:, pl.ds(y * C, C)] = weight[y]
        result = jnp.dot(values[...], wide[...], preferred_element_type=F32).astype(BF)
        feature = core if which == 0 else 1 - core
        for r in range(8):
            for y in range(4):
                out[r * 4 + y, feature] = result[r * 32 : r * 32 + 32, y * C : y * C + C]


def embed(received, own, other, later_own, later_other):
    vmem = pl.BlockSpec(memory_space=pltpu.VMEM)
    unread = pl.BlockSpec(memory_space=pl.ANY)
    return pl.pallas_call(
        embed_kernel,
        in_specs=[vmem, vmem, vmem, unread, unread],
        out_shape=jax.ShapeDtypeStruct((32, 2, 32, C), BF),
        scratch_shapes=[
            pltpu.VMEM((2048, C), F32),
            pltpu.VMEM((256, 1024), BF),
            pltpu.VMEM((1024, 512), BF),
        ],
        compiler_params=params(),
        name="embed",
    )(received, own, other, later_own, later_other)


def sum_kernel(copies, terms, *rest):
    out, total_out = rest[-2:]
    total = terms[0].astype(F32)
    for i in range(1, terms.shape[0]):
        total = total + terms[i].astype(F32)
    if len(rest) == 3:
        total = rest[0][...].astype(F32) + total
    total = total.astype(BF)
    total_out[...] = total
    for i in range(copies):
        out[i] = total


def sum_and_copy(copies, terms, *base):
    return pl.pallas_call(
        functools.partial(sum_kernel, copies),
        out_shape=[
            jax.ShapeDtypeStruct((copies, 2, 32, C), BF),
            jax.ShapeDtypeStruct((2, 32, C), BF),
        ],
        compiler_params=params(),
        name="sum_and_copy",
    )(terms, *base)


def qkv_kernel(embedded, weight, queries, pairs):
    normed = []
    for core in range(2):
        blocks = [
            embedded[pair * 2 + core, feature].astype(F32)
            for pair in range(8)
            for feature in range(2)
        ]
        square = sum(block * block for block in blocks)
        square = jnp.sum(square, axis=-1, keepdims=True)
        scale = lax.rsqrt(square * (1.0 / 2048.0) + EPS)
        normed.append(jnp.concatenate([(block * scale).astype(BF) for block in blocks], axis=1))
    normed = jnp.concatenate(normed, axis=0)
    queries[...] = jnp.dot(normed, weight[0], preferred_element_type=F32).astype(BF)
    for part in range(2):
        result = jnp.dot(normed, weight[1 + part], preferred_element_type=F32).astype(BF)
        for r in range(8):
            pairs[r, part] = result


def project_qkv(embedded, weight):
    return pl.pallas_call(
        qkv_kernel,
        out_shape=[
            jax.ShapeDtypeStruct((64, C), BF),
            jax.ShapeDtypeStruct((8, 2, 64, C), BF),
        ],
        compiler_params=params(),
        name="qkv",
    )(embedded, weight)


def attend_kernel(queries, pairs, weight, out):
    keys = pairs[:, 0].reshape(512, C)
    values = pairs[:, 1].reshape(512, C)
    scores = lax.dot_general(
        queries[...], keys, (((1,), (1,)), ((), ())), preferred_element_type=F32
    ) * C ** (-0.5)
    scores = jnp.exp(scores - jnp.max(scores, axis=-1, keepdims=True))
    weights = (scores / jnp.sum(scores, axis=-1, keepdims=True)).astype(BF)
    attended = jnp.dot(weights, values, preferred_element_type=F32).astype(BF)
    projected = jnp.dot(attended, weight[...], preferred_element_type=F32).astype(BF)
    for pair in range(8):
        for core in range(2):
            for feature in range(2):
                at = (pair * 2 + feature) * C
                out[pair * 2 + core, feature] = projected[core * 32 : core * 32 + 32, at : at + C]


def attend(queries, pairs, weight):
    return pl.pallas_call(
        attend_kernel,
        out_shape=jax.ShapeDtypeStruct((16, 2, 32, C), BF),
        compiler_params=params(),
        name="attend",
    )(queries, pairs, weight)


def unembed_kernel(mixed, own, other, out, values, wide, rows):
    core = lax.axis_index("core")
    for which, weight in enumerate((own, other)):
        feature = core if which == 0 else 1 - core
        for y in range(4):
            at = pl.ds((which * 4 + y) * C, C)
            wide[:, at] = weight[y]
            for r in range(8):
                values[pl.ds(r * 32, 32), at] = mixed[r * 4 + y, feature]
    for j in range(8):
        rows[pl.ds(j, 256, stride=8), :] = lax.dot_general(
            values[...],
            wide[pl.ds(j * C, C), :],
            (((1,), (1,)), ((), ())),
            preferred_element_type=F32,
        )
    out[...] = rows[...].astype(BF).reshape(64, 32, C)


def unembed(mixed, own, other):
    return pl.pallas_call(
        unembed_kernel,
        out_shape=jax.ShapeDtypeStruct((64, 32, C), BF),
        scratch_shapes=[
            pltpu.VMEM((256, 1024), BF),
            pltpu.VMEM((1024, 1024), BF),
            pltpu.VMEM((2048, C), F32),
        ],
        compiler_params=params(),
        name="unembed",
    )(mixed, own, other)


def finish_kernel(features, received, out, patch, spread):
    frame, step = pl.program_id(0), pl.program_id(1)

    @pl.when((frame == 0) & (step == 0))
    def _():
        for r in range(8):
            for y in range(4):
                total = received[r * 8 + y].astype(F32) + received[r * 8 + 4 + y].astype(F32)
                patch[r * 4 + y] = total.astype(BF).astype(F32)

    token = frame * 2 + step // 2
    at = pl.ds(pl.multiple_of(token * 8, 8), 8)
    for q in range(CHUNK // 4):
        piece = ((step % 2) * 4 + q // 2) * 4 + (q % 2) * 2
        small = jnp.concatenate([patch[piece, at, :], patch[piece + 1, at, :]], axis=0)
        for row in range(4):
            for m in range(4):
                value = features[0, q * 4 + row, m].astype(F32) + small
                spread[q * 4 + row, pl.ds(m, 16, stride=4), :] = value
    out[0] = spread[...].astype(BF)


def finish(features, received):
    return pl.pallas_call(
        finish_kernel,
        grid=(2, 128 // CHUNK),
        in_specs=[
            pl.BlockSpec((1, CHUNK, 4, 16, C), lambda f, i: (f, i, 0, 0, 0)),
            whole((64, 32, C)),
        ],
        out_specs=pl.BlockSpec((1, CHUNK, 64, C), lambda f, i: (f, i, 0, 0)),
        out_shape=jax.ShapeDtypeStruct((2, 128, 64, C), BF),
        scratch_shapes=[
            pltpu.VMEM((32, 32, C), F32),
            pltpu.VMEM((CHUNK, 64, C), F32),
        ],
        compiler_params=params(),
        name="finish",
    )(features, received)


def exchange(array, axes):
    return lax.all_to_all(array, axes, 0, 0, tiled=True)


def from_neighbours(low, high, axes, count):
    forward = [(i, i + 1) for i in range(count - 1)]
    backward = [(i + 1, i) for i in range(count - 1)]
    return lax.ppermute(low, axes, forward), lax.ppermute(high, axes, backward)


def on_device(frames, conv_weight, embed_weight, unembed_weight, qkv_weight, out_weight):
    top, bottom = from_neighbours(frames[:, 127:], frames[:, :1], ROW, 8)
    edges = [
        jnp.concatenate([top[:, :, x], frames[:, :, x], bottom[:, :, x]], axis=1) for x in (63, 0)
    ]
    left, right = from_neighbours(edges[0], edges[1], COL, 16)
    embed_own = exchange(embed_weight.reshape(4, 1024, C), "y")
    unembed_own = exchange(unembed_weight.reshape(4, 1024, C), "y")
    swap = [(0, 1), (1, 0)]
    embed_other = lax.ppermute(embed_own, "core", swap)
    unembed_other = lax.ppermute(unembed_own, "core", swap)
    features, patches = convolve(
        frames, top, bottom, left.astype(F32), right.astype(F32), conv_weight
    )
    partial = embed(
        exchange(patches, SAME), embed_own, embed_other, unembed_own, unembed_other
    )
    copies, embedded = sum_and_copy(16, exchange(partial, ROWY))
    queries, pairs = project_qkv(exchange(copies, COL), qkv_weight)
    projected = attend(queries, exchange(pairs, ROW), out_weight)
    copies, _ = sum_and_copy(32, exchange(projected, COL), embedded)
    patch_values = unembed(exchange(copies, ROWY), unembed_own, unembed_other)
    return finish(features, exchange(patch_values, SAME))


def solution(mesh):
    fine = jax.sharding.Mesh(mesh.devices.reshape(4, 2, 2, 4, 2), EVERY)
    placed = (
        P(None, ROW, COL, None),
        P(),
        P(ROW, COL),
        P(ROW, COL),
        P(None, None, COL),
        P(COL, None),
    )
    return jax.shard_map(
        on_device,
        mesh=fine,
        in_specs=placed,
        out_specs=P(None, ROW, COL, None),
        check_vma=False,
    )
```

```python
import functools

import jax
import jax.numpy as jnp
from jax import lax
from jax.experimental import pallas as pl
from jax.experimental.pallas import tpu as pltpu
from jax.sharding import PartitionSpec as P

C = 128
BF = jnp.bfloat16
F32 = jnp.float32
EPS = 1e-06
ROW = ("z", "xl")
COL = ("xh", "y", "core")
ROWY = ROW + ("y",)
SAME = ROW + ("xh", "y")
EVERY = ROW + COL
CHUNK = 64
SPREAD = 32
SUB = 16
LEFT = 8


def params(mib=24):
    return pltpu.CompilerParams(vmem_limit_bytes=mib * 2**20)


def near(*arrays):
    return [pltpu.with_memory_space_constraint(array, pltpu.VMEM) for array in arrays]


VMEM = pl.BlockSpec(memory_space=pltpu.VMEM)


def conv_kernel(
    frames, top, bottom, left, right, weight, features, send, padded, taps, kernel, pooled
):
    frame, step = pl.program_id(0), pl.program_id(1)
    steps = pl.num_programs(1)

    @pl.when((frame == 0) & (step == 0))
    def _():
        for a in range(3):
            for k in range(4):
                for o in range(2):
                    b = k - o
                    block = weight[a, b] if 0 <= b <= 2 else jnp.zeros((C, C), BF)
                    kernel[pl.ds(a * 512 + k * C, C), pl.ds(o * C, C)] = block

    cols = pl.ds(LEFT, 64)
    start = step * CHUNK
    padded[pl.ds(1, CHUNK), cols, :] = frames[frame, pl.ds(start, CHUNK)].astype(F32)
    above = frames[frame, jnp.maximum(start - 1, 0)].astype(F32)
    padded[0, cols, :] = jnp.where(step == 0, top[frame, 0].astype(F32), above)
    below = frames[frame, jnp.minimum(start + CHUNK, 127)].astype(F32)
    padded[CHUNK + 1, cols, :] = jnp.where(step == steps - 1, bottom[frame, 0].astype(F32), below)
    rows = pl.ds(pl.multiple_of(start, CHUNK), CHUNK + 2)
    padded[:, LEFT - 1, :] = left[frame, rows, :].astype(F32)
    padded[:, LEFT + 64, :] = right[frame, rows, :].astype(F32)
    for k in range(6):
        taps[:, :, pl.ds(k * C, C)] = padded[:, pl.ds(LEFT - 1 + k, 16, stride=4), :].astype(BF)

    for sub in range(CHUNK // SUB):
        total = jnp.zeros((SUB // 4, 16, C), F32)
        for pair in range(2):
            lhs = jnp.concatenate(
                [
                    taps[pl.ds(sub * SUB + a, SUB), :, pl.ds(pair * 256, 512)].reshape(SUB * 16, 512)
                    for a in range(3)
                ],
                axis=1,
            )
            result = jnp.dot(lhs, kernel[...], preferred_element_type=F32)
            for o in range(2):
                m = pair * 2 + o
                v = result[:, o * C : (o + 1) * C]
                mean = jnp.mean(v * v, axis=-1, keepdims=True)
                h = v * (0.5 * lax.rsqrt(mean + EPS))
                x = taps[pl.ds(sub * SUB + 1, SUB), :, pl.ds((m + 1) * C, C)].reshape(SUB * 16, C)
                f = x.astype(F32) + (h + h * jnp.tanh(h))
                f = f.reshape(SUB, 16, C)
                features[frame, pl.ds(step * CHUNK + sub * SUB, SUB), m] = f.astype(BF)
                total = total + f.reshape(SUB // 4, 4, 16, C).sum(axis=1)
        mean = total * (1.0 / 16.0)
        for g in range(SUB // 4):
            q = sub * (SUB // 4) + g
            token = frame * 2 + step
            for half in range(2):
                piece = q * 2 + half
                at = pl.ds(pl.multiple_of(token * 8, 8), 8)
                pooled[piece, at, :] = mean[g, half * 8 : half * 8 + 8]

    @pl.when((frame == 1) & (step == steps - 1))
    def _():
        for r in range(8):
            for y in range(4):
                block = pooled[r * 4 + y].astype(BF)
                for xh in range(2):
                    send[(r * 2 + xh) * 4 + y] = block


def convolve(frames, top, bottom, left, right, weight):
    steps = 128 // CHUNK
    return pl.pallas_call(
        conv_kernel,
        grid=(2, steps),
        in_specs=[VMEM] * 6,
        out_specs=[VMEM, VMEM],
        out_shape=[pltpu.VMEM((2, 128, 4, 16, C), BF), pltpu.VMEM((64, 32, C), BF)],
        scratch_shapes=[
            pltpu.VMEM((CHUNK + 2, 80, C), F32),
            pltpu.VMEM((CHUNK + 2, 16, 6 * C), BF),
            pltpu.VMEM((3 * 512, 2 * C), BF),
            pltpu.VMEM((32, 32, C), F32),
        ],
        compiler_params=params(),
        cost_estimate=pl.CostEstimate(
            flops=2 * 16384 * 9 * C * C, bytes_accessed=9 * 2**20, transcendentals=2 * 16384 * C
        ),
        name="conv_block",
    )(*near(frames, top, bottom, left, right, weight))


def embed_kernel(received, own, other, out, rows, values, wide):
    core = lax.axis_index("core")
    rows[...] = received[...].reshape(2048, C).astype(F32)
    for j in range(8):
        values[:, pl.ds(j * C, C)] = rows[pl.ds(j, 256, stride=8), :].astype(BF)
    for which, weight in enumerate((own, other)):
        for y in range(4):
            wide[:, pl.ds(y * C, C)] = weight[y, pl.ds(0, 1024)]
        result = jnp.dot(values[...], wide[...], preferred_element_type=F32).astype(BF)
        feature = core if which == 0 else 1 - core
        for r in range(8):
            for y in range(4):
                out[r * 4 + y, feature] = result[r * 32 : r * 32 + 32, y * C : y * C + C]


def embed(received, own, other):
    return pl.pallas_call(
        embed_kernel,
        out_shape=pltpu.VMEM((32, 2, 32, C), BF),
        scratch_shapes=[
            pltpu.VMEM((2048, C), F32),
            pltpu.VMEM((256, 1024), BF),
            pltpu.VMEM((1024, 512), BF),
        ],
        compiler_params=params(),
        name="embed",
    )(*near(received, own, other))


def sum_kernel(copies, terms, *rest):
    out, total_out = rest[-2:]
    total = terms[0].astype(F32)
    for i in range(1, terms.shape[0]):
        total = total + terms[i].astype(F32)
    if len(rest) == 3:
        total = rest[0][...].astype(F32) + total
    total = total.astype(BF)
    total_out[...] = total
    for i in range(copies):
        out[i] = total


def sum_and_copy(copies, terms, *base):
    return pl.pallas_call(
        functools.partial(sum_kernel, copies),
        out_shape=[pltpu.VMEM((copies, 2, 32, C), BF), pltpu.VMEM((2, 32, C), BF)],
        compiler_params=params(),
        name="sum_and_copy",
    )(*near(terms, *base))


def qkv_kernel(embedded, weight, queries, pairs):
    normed = []
    for core in range(2):
        blocks = [
            embedded[pair * 2 + core, feature].astype(F32)
            for pair in range(8)
            for feature in range(2)
        ]
        square = sum(block * block for block in blocks)
        square = jnp.sum(square, axis=-1, keepdims=True)
        scale = lax.rsqrt(square * (1.0 / 2048.0) + EPS)
        normed.append(jnp.concatenate([(block * scale).astype(BF) for block in blocks], axis=1))
    normed = jnp.concatenate(normed, axis=0)
    queries[...] = jnp.dot(normed, weight[0], preferred_element_type=F32).astype(BF)
    for part in range(2):
        result = jnp.dot(normed, weight[1 + part], preferred_element_type=F32).astype(BF)
        for r in range(8):
            pairs[r, part] = result


def project_qkv(embedded, weight):
    return pl.pallas_call(
        qkv_kernel,
        out_shape=[pltpu.VMEM((64, C), BF), pltpu.VMEM((8, 2, 64, C), BF)],
        compiler_params=params(),
        name="qkv",
    )(*near(embedded, weight))


def attend_kernel(queries, pairs, weight, out):
    keys = pairs[:, 0].reshape(512, C)
    values = pairs[:, 1].reshape(512, C)
    scores = lax.dot_general(
        queries[...], keys, (((1,), (1,)), ((), ())), preferred_element_type=F32
    ) * C ** (-0.5)
    scores = jnp.exp(scores - jnp.max(scores, axis=-1, keepdims=True))
    weights = (scores / jnp.sum(scores, axis=-1, keepdims=True)).astype(BF)
    attended = jnp.dot(weights, values, preferred_element_type=F32).astype(BF)
    projected = jnp.dot(attended, weight[...], preferred_element_type=F32).astype(BF)
    for pair in range(8):
        for core in range(2):
            for feature in range(2):
                at = (pair * 2 + feature) * C
                out[pair * 2 + core, feature] = projected[core * 32 : core * 32 + 32, at : at + C]


def attend(queries, pairs, weight):
    return pl.pallas_call(
        attend_kernel,
        out_shape=pltpu.VMEM((16, 2, 32, C), BF),
        compiler_params=params(),
        name="attend",
    )(*near(queries, pairs, weight))


def unembed_kernel(mixed, own, other, out, values, wide, rows):
    core = lax.axis_index("core")
    for which, weight in enumerate((own, other)):
        feature = core if which == 0 else 1 - core
        for y in range(4):
            at = pl.ds((which * 4 + y) * C, C)
            wide[:, at] = weight[y, pl.ds(1024, 1024)]
            for r in range(8):
                values[pl.ds(r * 32, 32), at] = mixed[r * 4 + y, feature]
    for j in range(8):
        rows[pl.ds(j, 256, stride=8), :] = lax.dot_general(
            values[...],
            wide[pl.ds(j * C, C), :],
            (((1,), (1,)), ((), ())),
            preferred_element_type=F32,
        )
    out[...] = rows[...].astype(BF).reshape(64, 32, C)


def unembed(mixed, own, other):
    return pl.pallas_call(
        unembed_kernel,
        out_shape=pltpu.VMEM((64, 32, C), BF),
        scratch_shapes=[
            pltpu.VMEM((256, 1024), BF),
            pltpu.VMEM((1024, 1024), BF),
            pltpu.VMEM((2048, C), F32),
        ],
        compiler_params=params(),
        name="unembed",
    )(*near(mixed, own, other))


def finish_kernel(features, received, out, patch, spread):
    frame, step = pl.program_id(0), pl.program_id(1)

    @pl.when((frame == 0) & (step == 0))
    def _():
        for r in range(8):
            for y in range(4):
                total = received[r * 8 + y].astype(F32) + received[r * 8 + 4 + y].astype(F32)
                patch[r * 4 + y] = total.astype(BF).astype(F32)

    token = frame * 2 + step // 2
    at = pl.ds(pl.multiple_of(token * 8, 8), 8)
    for q in range(SPREAD // 4):
        piece = ((step % 2) * 4 + q // 2) * 4 + (q % 2) * 2
        small = jnp.concatenate([patch[piece, at, :], patch[piece + 1, at, :]], axis=0)
        for row in range(4):
            for m in range(4):
                value = features[frame, step * SPREAD + q * 4 + row, m].astype(F32) + small
                spread[q * 4 + row, pl.ds(m, 16, stride=4), :] = value
    out[0] = spread[...].astype(BF)


def finish(features, received):
    return pl.pallas_call(
        finish_kernel,
        grid=(2, 128 // SPREAD),
        in_specs=[VMEM, VMEM],
        out_specs=pl.BlockSpec((1, SPREAD, 64, C), lambda f, i: (f, i, 0, 0)),
        out_shape=jax.ShapeDtypeStruct((2, 128, 64, C), BF),
        scratch_shapes=[
            pltpu.VMEM((32, 32, C), F32),
            pltpu.VMEM((SPREAD, 64, C), F32),
        ],
        compiler_params=params(),
        name="finish",
    )(*near(features, received))


def exchange(array, axes):
    return lax.all_to_all(array, axes, 0, 0, tiled=True)


def from_neighbours(low, high, axes, count):
    forward = [(i, i + 1) for i in range(count - 1)]
    backward = [(i + 1, i) for i in range(count - 1)]
    return lax.ppermute(low, axes, forward), lax.ppermute(high, axes, backward)


def on_device(frames, conv_weight, embed_weight, unembed_weight, qkv_weight, out_weight):
    top, bottom = from_neighbours(frames[:, 127:], frames[:, :1], ROW, 8)
    edges = [
        jnp.concatenate([top[:, :, x], frames[:, :, x], bottom[:, :, x]], axis=1) for x in (63, 0)
    ]
    left, right = from_neighbours(edges[0], edges[1], COL, 16)
    both = [weight.reshape(4, 1024, C) for weight in (embed_weight, unembed_weight)]
    own = exchange(jnp.concatenate(both, axis=1), "y")
    features, patches = convolve(frames, top, bottom, left, right, conv_weight)
    own, patches = lax.optimization_barrier((own, patches))
    other = lax.ppermute(own, "core", [(0, 1), (1, 0)])
    partial = embed(exchange(patches, SAME), own, other)
    copies, embedded = sum_and_copy(16, exchange(partial, ROWY))
    queries, pairs = project_qkv(exchange(copies, COL), qkv_weight)
    projected = attend(queries, exchange(pairs, ROW), out_weight)
    copies, _ = sum_and_copy(32, exchange(projected, COL), embedded)
    patch_values = unembed(exchange(copies, ROWY), own, other)
    return finish(features, exchange(patch_values, SAME))


def solution(mesh):
    fine = jax.sharding.Mesh(mesh.devices.reshape(4, 2, 2, 4, 2), EVERY)
    placed = (
        P(None, ROW, COL, None),
        P(),
        P(ROW, COL),
        P(ROW, COL),
        P(None, None, COL),
        P(COL, None),
    )
    return jax.shard_map(
        on_device,
        mesh=fine,
        in_specs=placed,
        out_specs=P(None, ROW, COL, None),
        check_vma=False,
    )
```

```python
import functools

import jax
import jax.numpy as jnp
from jax import lax
from jax.experimental import pallas as pl
from jax.experimental.pallas import tpu as pltpu
from jax.sharding import PartitionSpec as P

C = 128
BF = jnp.bfloat16
F32 = jnp.float32
EPS = 1e-06
ROW = ("z", "xl")
COL = ("xh", "y", "core")
ROWY = ROW + ("y",)
SAME = ROW + ("xh", "y")
EVERY = ROW + COL
CHUNK = 64
SPREAD = 64
SUB = 16
LEFT = 8


def params(mib=12):
    return pltpu.CompilerParams(vmem_limit_bytes=mib * 2**20)


def near(*arrays):
    return [pltpu.with_memory_space_constraint(array, pltpu.VMEM) for array in arrays]


VMEM = pl.BlockSpec(memory_space=pltpu.VMEM)


def conv_kernel(
    main, above, below, top, bottom, left, right, weight, features, send, padded, taps, kernel, pooled
):
    frame, step = pl.program_id(0), pl.program_id(1)

    @pl.when((frame == 0) & (step == 0))
    def _():
        for a in range(3):
            for k in range(4):
                for o in range(2):
                    b = k - o
                    block = weight[a, b] if 0 <= b <= 2 else jnp.zeros((C, C), BF)
                    kernel[pl.ds(a * 512 + k * C, C), pl.ds(o * C, C)] = block

    cols = pl.ds(LEFT, 64)
    start = step * CHUNK
    padded[pl.ds(1, CHUNK), cols, :] = main[0].astype(F32)
    rows = pl.ds(pl.multiple_of(start, CHUNK), CHUNK)
    padded[pl.ds(1, CHUNK), LEFT - 1, :] = left[frame, rows, :].astype(F32)
    padded[pl.ds(1, CHUNK), LEFT + 64, :] = right[frame, rows, :].astype(F32)
    for border, outside, inside, row, at in (
        (step == 0, top, above, CHUNK - 1, 0),
        (step == 1, bottom, below, CHUNK, CHUNK + 1),
    ):

        @pl.when(border)
        def _(outside=outside, at=at):
            padded[at, cols, :] = outside[frame, pl.ds(0, 64)].astype(F32)
            corners = outside[frame, pl.ds(64, 16)].astype(F32)
            padded[at, pl.ds(LEFT - 1, 1), :] = corners[:1]
            padded[at, pl.ds(LEFT + 64, 1), :] = corners[1:2]

        @pl.when(jnp.logical_not(border))
        def _(inside=inside, row=row, at=at):
            padded[at, cols, :] = inside[0, 0].astype(F32)
            near_row = pl.ds(row // 16 * 16, 16)
            for side, col in ((left, LEFT - 1), (right, LEFT + 64)):
                value = side[frame, near_row, :].astype(F32)
                padded[at, pl.ds(col, 1), :] = value[row % 16 : row % 16 + 1]

    for k in range(6):
        taps[:, :, pl.ds(k * C, C)] = padded[:, pl.ds(LEFT - 1 + k, 16, stride=4), :].astype(BF)

    for sub in range(CHUNK // SUB):
        total = jnp.zeros((SUB // 4, 16, C), F32)
        for pair in range(2):
            lhs = jnp.concatenate(
                [
                    taps[pl.ds(sub * SUB + a, SUB), :, pl.ds(pair * 256, 512)].reshape(SUB * 16, 512)
                    for a in range(3)
                ],
                axis=1,
            )
            result = jnp.dot(lhs, kernel[...], preferred_element_type=F32)
            for o in range(2):
                m = pair * 2 + o
                v = result[:, o * C : (o + 1) * C]
                mean = jnp.mean(v * v, axis=-1, keepdims=True)
                h = v * (0.5 * lax.rsqrt(mean + EPS))
                x = taps[pl.ds(sub * SUB + 1, SUB), :, pl.ds((m + 1) * C, C)].reshape(SUB * 16, C)
                f = x.astype(F32) + (h + h * jnp.tanh(h))
                f = f.reshape(SUB, 16, C)
                features[0, pl.ds(sub * SUB, SUB), m] = f.astype(BF)
                total = total + f.reshape(SUB // 4, 4, 16, C).sum(axis=1)
        mean = total * (1.0 / 16.0)
        for g in range(SUB // 4):
            q = sub * (SUB // 4) + g
            token = frame * 2 + step
            for half in range(2):
                piece = q * 2 + half
                at = pl.ds(pl.multiple_of(token * 8, 8), 8)
                pooled[piece, at, :] = mean[g, half * 8 : half * 8 + 8]

    @pl.when((frame == 1) & (step == 1))
    def _():
        for r in range(8):
            for y in range(4):
                block = pooled[r * 4 + y].astype(BF)
                for xh in range(2):
                    send[(r * 2 + xh) * 4 + y] = block


def convolve(frames, top, bottom, left, right, weight):
    steps = 128 // CHUNK
    far = pltpu.with_memory_space_constraint(frames, pltpu.HBM)
    return pl.pallas_call(
        conv_kernel,
        grid=(2, steps),
        in_specs=[
            pl.BlockSpec((1, CHUNK, 64, C), lambda f, i: (f, i, 0, 0)),
            pl.BlockSpec((1, 1, 64, C), lambda f, i: (f, CHUNK - 1, 0, 0)),
            pl.BlockSpec((1, 1, 64, C), lambda f, i: (f, CHUNK, 0, 0)),
        ]
        + [VMEM] * 5,
        out_specs=[pl.BlockSpec((1, CHUNK, 4, 16, C), lambda f, i: (f, i, 0, 0, 0)), VMEM],
        out_shape=[
            pltpu.HBM((2, 128, 4, 16, C), BF),
            pltpu.VMEM((64, 32, C), BF),
        ],
        scratch_shapes=[
            pltpu.VMEM((CHUNK + 2, 80, C), F32),
            pltpu.VMEM((CHUNK + 2, 16, 6 * C), BF),
            pltpu.VMEM((3 * 512, 2 * C), BF),
            pltpu.VMEM((32, 32, C), F32),
        ],
        compiler_params=params(),
        cost_estimate=pl.CostEstimate(
            flops=2 * 16384 * 9 * C * C, bytes_accessed=9 * 2**20, transcendentals=2 * 16384 * C
        ),
        name="conv_block",
    )(far, far, far, *near(top, bottom, left, right, weight))


def embed_kernel(received, own, other, out, rows, values, wide):
    core = lax.axis_index("core")
    rows[...] = received[...].reshape(2048, C).astype(F32)
    for j in range(8):
        values[:, pl.ds(j * C, C)] = rows[pl.ds(j, 256, stride=8), :].astype(BF)
    for which, weight in enumerate((own, other)):
        for y in range(4):
            wide[:, pl.ds(y * C, C)] = weight[y, pl.ds(0, 1024)]
        result = jnp.dot(values[...], wide[...], preferred_element_type=F32).astype(BF)
        feature = core if which == 0 else 1 - core
        for r in range(8):
            for y in range(4):
                out[r * 4 + y, feature] = result[r * 32 : r * 32 + 32, y * C : y * C + C]


def embed(received, own, other):
    return pl.pallas_call(
        embed_kernel,
        out_shape=pltpu.VMEM((32, 2, 32, C), BF),
        scratch_shapes=[
            pltpu.VMEM((2048, C), F32),
            pltpu.VMEM((256, 1024), BF),
            pltpu.VMEM((1024, 512), BF),
        ],
        compiler_params=params(),
        name="embed",
    )(*near(received, own, other))


def sum_kernel(copies, terms, *rest):
    out, total_out = rest[-2:]
    total = terms[0].astype(F32)
    for i in range(1, terms.shape[0]):
        total = total + terms[i].astype(F32)
    if len(rest) == 3:
        total = rest[0][...].astype(F32) + total
    total = total.astype(BF)
    total_out[...] = total
    for i in range(copies):
        out[i] = total


def sum_and_copy(copies, terms, *base):
    return pl.pallas_call(
        functools.partial(sum_kernel, copies),
        out_shape=[pltpu.VMEM((copies, 2, 32, C), BF), pltpu.VMEM((2, 32, C), BF)],
        compiler_params=params(),
        name="sum_and_copy",
    )(*near(terms, *base))


def qkv_kernel(embedded, weight, queries, pairs):
    normed = []
    for core in range(2):
        blocks = [
            embedded[pair * 2 + core, feature].astype(F32)
            for pair in range(8)
            for feature in range(2)
        ]
        square = sum(block * block for block in blocks)
        square = jnp.sum(square, axis=-1, keepdims=True)
        scale = lax.rsqrt(square * (1.0 / 2048.0) + EPS)
        normed.append(jnp.concatenate([(block * scale).astype(BF) for block in blocks], axis=1))
    normed = jnp.concatenate(normed, axis=0)
    queries[...] = jnp.dot(normed, weight[0], preferred_element_type=F32).astype(BF)
    for part in range(2):
        result = jnp.dot(normed, weight[1 + part], preferred_element_type=F32).astype(BF)
        for r in range(8):
            pairs[r, part] = result


def project_qkv(embedded, weight):
    return pl.pallas_call(
        qkv_kernel,
        out_shape=[pltpu.VMEM((64, C), BF), pltpu.VMEM((8, 2, 64, C), BF)],
        compiler_params=params(),
        name="qkv",
    )(*near(embedded, weight))


def attend_kernel(queries, pairs, weight, out):
    keys = pairs[:, 0].reshape(512, C)
    values = pairs[:, 1].reshape(512, C)
    scores = lax.dot_general(
        queries[...], keys, (((1,), (1,)), ((), ())), preferred_element_type=F32
    ) * C ** (-0.5)
    scores = jnp.exp(scores - jnp.max(scores, axis=-1, keepdims=True))
    weights = (scores / jnp.sum(scores, axis=-1, keepdims=True)).astype(BF)
    attended = jnp.dot(weights, values, preferred_element_type=F32).astype(BF)
    projected = jnp.dot(attended, weight[...], preferred_element_type=F32).astype(BF)
    for pair in range(8):
        for core in range(2):
            for feature in range(2):
                at = (pair * 2 + feature) * C
                out[pair * 2 + core, feature] = projected[core * 32 : core * 32 + 32, at : at + C]


def attend(queries, pairs, weight):
    return pl.pallas_call(
        attend_kernel,
        out_shape=pltpu.VMEM((16, 2, 32, C), BF),
        compiler_params=params(),
        name="attend",
    )(*near(queries, pairs, weight))


def unembed_kernel(mixed, own, other, out, values, wide, rows):
    core = lax.axis_index("core")
    for which, weight in enumerate((own, other)):
        feature = core if which == 0 else 1 - core
        for y in range(4):
            at = pl.ds((which * 4 + y) * C, C)
            wide[:, at] = weight[y, pl.ds(1024, 1024)]
            for r in range(8):
                values[pl.ds(r * 32, 32), at] = mixed[r * 4 + y, feature]
    for j in range(8):
        rows[pl.ds(j, 256, stride=8), :] = lax.dot_general(
            values[...],
            wide[pl.ds(j * C, C), :],
            (((1,), (1,)), ((), ())),
            preferred_element_type=F32,
        )
    out[...] = rows[...].astype(BF).reshape(64, 32, C)


def unembed(mixed, own, other):
    return pl.pallas_call(
        unembed_kernel,
        out_shape=pltpu.VMEM((64, 32, C), BF),
        scratch_shapes=[
            pltpu.VMEM((256, 1024), BF),
            pltpu.VMEM((1024, 1024), BF),
            pltpu.VMEM((2048, C), F32),
        ],
        compiler_params=params(),
        name="unembed",
    )(*near(mixed, own, other))


def finish_kernel(features, received, out, patch, spread):
    frame, step = pl.program_id(0), pl.program_id(1)

    @pl.when((frame == 0) & (step == 0))
    def _():
        for r in range(8):
            for y in range(4):
                total = received[r * 8 + y].astype(F32) + received[r * 8 + 4 + y].astype(F32)
                patch[r * 4 + y] = total.astype(BF).astype(F32)

    token = frame * 2 + step
    at = pl.ds(pl.multiple_of(token * 8, 8), 8)
    for q in range(SPREAD // 4):
        piece = q * 2
        small = jnp.concatenate([patch[piece, at, :], patch[piece + 1, at, :]], axis=0)
        for row in range(4):
            for m in range(4):
                value = features[frame, step * SPREAD + q * 4 + row, m].astype(F32) + small
                spread[q * 4 + row, pl.ds(m, 16, stride=4), :] = value
    out[0] = spread[...].astype(BF)


def finish(features, received):
    return pl.pallas_call(
        finish_kernel,
        grid=(2, 128 // SPREAD),
        in_specs=[VMEM, VMEM],
        out_specs=pl.BlockSpec((1, SPREAD, 64, C), lambda f, i: (f, i, 0, 0)),
        out_shape=jax.ShapeDtypeStruct((2, 128, 64, C), BF),
        scratch_shapes=[
            pltpu.VMEM((32, 32, C), F32),
            pltpu.VMEM((SPREAD, 64, C), F32),
        ],
        compiler_params=params(),
        name="finish",
    )(*near(features, received))


def exchange(array, axes):
    return lax.all_to_all(array, axes, 0, 0, tiled=True)


def from_neighbours(low, high, axes, count):
    forward = [(i, i + 1) for i in range(count - 1)]
    backward = [(i + 1, i) for i in range(count - 1)]
    return lax.ppermute(low, axes, forward), lax.ppermute(high, axes, backward)


def on_device(frames, conv_weight, embed_weight, unembed_weight, qkv_weight, out_weight):
    left, right = from_neighbours(frames[:, :, 63], frames[:, :, 0], COL, 16)
    both = [weight.reshape(4, 1024, C) for weight in (embed_weight, unembed_weight)]
    both = jnp.concatenate(both, axis=1)
    left, right, both = lax.optimization_barrier((left, right, both))
    rows = [
        jnp.pad(
            jnp.concatenate([frames[:, y], left[:, y : y + 1], right[:, y : y + 1]], axis=1),
            ((0, 0), (0, 14), (0, 0)),
        )
        for y in (127, 0)
    ]
    top, bottom = from_neighbours(rows[0], rows[1], ROW, 8)
    own = exchange(both, "y")
    features, patches = convolve(frames, top, bottom, left, right, conv_weight)
    own, patches = lax.optimization_barrier((own, patches))
    other = lax.ppermute(own, "core", [(0, 1), (1, 0)])
    partial = embed(exchange(patches, SAME), own, other)
    copies, embedded = sum_and_copy(16, exchange(partial, ROWY))
    queries, pairs = project_qkv(exchange(copies, COL), qkv_weight)
    projected = attend(queries, exchange(pairs, ROW), out_weight)
    copies, _ = sum_and_copy(32, exchange(projected, COL), embedded)
    patch_values = unembed(exchange(copies, ROWY), own, other)
    return finish(features, exchange(patch_values, SAME))


def solution(mesh):
    fine = jax.sharding.Mesh(mesh.devices.reshape(4, 2, 2, 4, 2), EVERY)
    placed = (
        P(None, ROW, COL, None),
        P(),
        P(ROW, COL),
        P(ROW, COL),
        P(None, None, COL),
        P(COL, None),
    )
    return jax.shard_map(
        on_device,
        mesh=fine,
        in_specs=placed,
        out_specs=P(None, ROW, COL, None),
        check_vma=False,
    )
```

```python
import functools

import jax
import jax.numpy as jnp
from jax import lax
from jax.experimental import pallas as pl
from jax.experimental.pallas import tpu as pltpu
from jax.sharding import PartitionSpec as P

C = 128
BF = jnp.bfloat16
F32 = jnp.float32
EPS = 1e-06
ROW = ("z", "xl")
COL = ("xh", "y", "core")
ROWY = ROW + ("y",)
PLANE = ("xh", "y")
SAME = ROW + PLANE
EVERY = ROW + COL
SWAP = [(0, 1), (1, 0)]
CHUNK = 64
SPREAD = 64
SUB = 16
LEFT = 8


def params(mib=12):
    return pltpu.CompilerParams(vmem_limit_bytes=mib * 2**20)


def near(*arrays):
    return [pltpu.with_memory_space_constraint(array, pltpu.VMEM) for array in arrays]


VMEM = pl.BlockSpec(memory_space=pltpu.VMEM)


def pack_kernel(first, second, both, held, arrived, left):
    pieces = [(i, y, part) for i, part in enumerate((first, second)) for y in range(4)]
    loads = [
        pltpu.make_async_copy(part.at[y], held.at[i, y], arrived.at[i, y])
        for i, y, part in pieces
    ]
    stores = [
        pltpu.make_async_copy(held.at[i, y], both.at[y, pl.ds(1024 * i, 1024)], left.at[i, y])
        for i, y, _ in pieces
    ]
    for copy in loads:
        copy.start()
    for load, store in zip(loads, stores):
        load.wait()
        store.start()
    for copy in stores:
        copy.wait()


def pack(first, second):
    hbm = pl.BlockSpec(memory_space=pltpu.HBM)
    return pl.pallas_call(
        pack_kernel,
        in_specs=[hbm] * 2,
        out_specs=hbm,
        out_shape=pltpu.HBM((4, 2048, C), BF),
        scratch_shapes=[
            pltpu.VMEM((2, 4, 1024, C), BF),
            pltpu.SemaphoreType.DMA((2, 4)),
            pltpu.SemaphoreType.DMA((2, 4)),
        ],
        compiler_params=params(),
        name="pack",
    )(*(pltpu.with_memory_space_constraint(a, pltpu.HBM) for a in (first, second)))


def conv_kernel(
    main, above, below, top, bottom, left, right, weight, features, send, padded, taps, kernel, pooled
):
    frame, step = pl.program_id(0), pl.program_id(1)

    @pl.when((frame == 0) & (step == 0))
    def _():
        for a in range(3):
            for k in range(4):
                for o in range(2):
                    b = k - o
                    block = weight[a, b] if 0 <= b <= 2 else jnp.zeros((C, C), BF)
                    kernel[pl.ds(a * 512 + k * C, C), pl.ds(o * C, C)] = block

    cols = pl.ds(LEFT, 64)
    start = step * CHUNK
    padded[pl.ds(1, CHUNK), cols, :] = main[0].astype(F32)
    rows = pl.ds(pl.multiple_of(start, CHUNK), CHUNK)
    padded[pl.ds(1, CHUNK), LEFT - 1, :] = left[frame, rows, :].astype(F32)
    padded[pl.ds(1, CHUNK), LEFT + 64, :] = right[frame, rows, :].astype(F32)
    for border, outside, inside, row, at in (
        (step == 0, top, above, CHUNK - 1, 0),
        (step == 1, bottom, below, CHUNK, CHUNK + 1),
    ):

        @pl.when(border)
        def _(outside=outside, at=at):
            padded[at, cols, :] = outside[frame, pl.ds(0, 64)].astype(F32)
            corners = outside[frame, pl.ds(64, 16)].astype(F32)
            padded[at, pl.ds(LEFT - 1, 1), :] = corners[:1]
            padded[at, pl.ds(LEFT + 64, 1), :] = corners[1:2]

        @pl.when(jnp.logical_not(border))
        def _(inside=inside, row=row, at=at):
            padded[at, cols, :] = inside[0, 0].astype(F32)
            near_row = pl.ds(row // 16 * 16, 16)
            for side, col in ((left, LEFT - 1), (right, LEFT + 64)):
                value = side[frame, near_row, :].astype(F32)
                padded[at, pl.ds(col, 1), :] = value[row % 16 : row % 16 + 1]

    for k in range(6):
        taps[:, :, pl.ds(k * C, C)] = padded[:, pl.ds(LEFT - 1 + k, 16, stride=4), :].astype(BF)

    for sub in range(CHUNK // SUB):
        total = jnp.zeros((SUB // 4, 16, C), F32)
        for pair in range(2):
            lhs = jnp.concatenate(
                [
                    taps[pl.ds(sub * SUB + a, SUB), :, pl.ds(pair * 256, 512)].reshape(SUB * 16, 512)
                    for a in range(3)
                ],
                axis=1,
            )
            result = jnp.dot(lhs, kernel[...], preferred_element_type=F32)
            for o in range(2):
                m = pair * 2 + o
                v = result[:, o * C : (o + 1) * C]
                mean = jnp.mean(v * v, axis=-1, keepdims=True)
                h = v * (0.5 * lax.rsqrt(mean + EPS))
                x = taps[pl.ds(sub * SUB + 1, SUB), :, pl.ds((m + 1) * C, C)].reshape(SUB * 16, C)
                f = x.astype(F32) + (h + h * jnp.tanh(h))
                f = f.reshape(SUB, 16, C)
                features[0, pl.ds(sub * SUB, SUB), m] = f.astype(BF)
                total = total + f.reshape(SUB // 4, 4, 16, C).sum(axis=1)
        mean = total * (1.0 / 16.0)
        for g in range(SUB // 4):
            q = sub * (SUB // 4) + g
            token = frame * 2 + step
            for half in range(2):
                piece = q * 2 + half
                at = pl.ds(pl.multiple_of(token * 8, 8), 8)
                pooled[piece, at, :] = mean[g, half * 8 : half * 8 + 8]

    @pl.when((frame == 1) & (step == 1))
    def _():
        for r in range(8):
            for y in range(4):
                block = pooled[r * 4 + y].astype(BF)
                for xh in range(2):
                    send[(r * 2 + xh) * 4 + y] = block


def convolve(frames, top, bottom, left, right, weight):
    steps = 128 // CHUNK
    far = pltpu.with_memory_space_constraint(frames, pltpu.HBM)
    return pl.pallas_call(
        conv_kernel,
        grid=(2, steps),
        in_specs=[
            pl.BlockSpec((1, CHUNK, 64, C), lambda f, i: (f, i, 0, 0)),
            pl.BlockSpec((1, 1, 64, C), lambda f, i: (f, CHUNK - 1, 0, 0)),
            pl.BlockSpec((1, 1, 64, C), lambda f, i: (f, CHUNK, 0, 0)),
        ]
        + [VMEM] * 5,
        out_specs=[pl.BlockSpec((1, CHUNK, 4, 16, C), lambda f, i: (f, i, 0, 0, 0)), VMEM],
        out_shape=[
            pltpu.HBM((2, 128, 4, 16, C), BF),
            pltpu.VMEM((64, 32, C), BF),
        ],
        scratch_shapes=[
            pltpu.VMEM((CHUNK + 2, 80, C), F32),
            pltpu.VMEM((CHUNK + 2, 16, 6 * C), BF),
            pltpu.VMEM((3 * 512, 2 * C), BF),
            pltpu.VMEM((32, 32, C), F32),
        ],
        compiler_params=params(),
        cost_estimate=pl.CostEstimate(
            flops=2 * 16384 * 9 * C * C, bytes_accessed=9 * 2**20, transcendentals=2 * 16384 * C
        ),
        name="conv_block",
    )(far, far, far, *near(top, bottom, left, right, weight))


def embed_kernel(received, own, other, out, rows, values):
    core = lax.axis_index("core")
    rows[...] = received[...].reshape(2048, C).astype(F32)
    for j in range(8):
        values[:, pl.ds(j * C, C)] = rows[pl.ds(j, 256, stride=8), :].astype(BF)
    for which, weight in enumerate((own, other)):
        wide = jnp.concatenate([weight[y, pl.ds(0, 1024)] for y in range(4)], axis=1)
        result = jnp.dot(values[...], wide, preferred_element_type=F32).astype(BF)
        feature = core if which == 0 else 1 - core
        for r in range(8):
            for y in range(4):
                out[r * 4 + y, feature] = result[r * 32 : r * 32 + 32, y * C : y * C + C]


def embed(received, own, other):
    return pl.pallas_call(
        embed_kernel,
        out_shape=pltpu.VMEM((32, 2, 32, C), BF),
        scratch_shapes=[
            pltpu.VMEM((2048, C), F32),
            pltpu.VMEM((256, 1024), BF),
        ],
        compiler_params=params(),
        name="embed",
    )(*near(received, own, other))


def sum_kernel(copies, terms, *rest):
    out, total_out = rest[-2:]
    total = terms[0].astype(F32)
    for i in range(1, terms.shape[0]):
        total = total + terms[i].astype(F32)
    if len(rest) == 3:
        total = rest[0][...].astype(F32) + total
    total = total.astype(BF)
    total_out[...] = total
    for i in range(copies):
        out[i] = total


def sum_and_copy(copies, terms, *base):
    return pl.pallas_call(
        functools.partial(sum_kernel, copies),
        out_shape=[pltpu.VMEM((copies, 2, 32, C), BF), pltpu.VMEM((2, 32, C), BF)],
        compiler_params=params(),
        name="sum_and_copy",
    )(*near(terms, *base))


def qkv_kernel(own, other, weight, queries, pairs):
    normed = []
    for group in (own, other):
        blocks = [group[pair, feature].astype(F32) for pair in range(8) for feature in range(2)]
        square = sum(block * block for block in blocks)
        square = jnp.sum(square, axis=-1, keepdims=True)
        scale = lax.rsqrt(square * (1.0 / 2048.0) + EPS)
        normed.append(jnp.concatenate([(block * scale).astype(BF) for block in blocks], axis=1))
    normed = jnp.concatenate(normed, axis=0)
    queries[...] = jnp.dot(normed, weight[0], preferred_element_type=F32).astype(BF)
    for part in range(2):
        result = jnp.dot(normed, weight[1 + part], preferred_element_type=F32).astype(BF)
        for r in range(8):
            pairs[r, part] = result


def project_qkv(own, other, weight):
    return pl.pallas_call(
        qkv_kernel,
        out_shape=[pltpu.VMEM((64, C), BF), pltpu.VMEM((8, 2, 64, C), BF)],
        compiler_params=params(),
        name="qkv",
    )(*near(own, other, weight))


def attend_kernel(queries, pairs, weight, out):
    keys = pairs[:, 0].reshape(512, C)
    values = pairs[:, 1].reshape(512, C)
    scores = lax.dot_general(
        queries[...], keys, (((1,), (1,)), ((), ())), preferred_element_type=F32
    ) * C ** (-0.5)
    scores = jnp.exp(scores - jnp.max(scores, axis=-1, keepdims=True))
    weights = (scores / jnp.sum(scores, axis=-1, keepdims=True)).astype(BF)
    attended = jnp.dot(weights, values, preferred_element_type=F32).astype(BF)
    projected = jnp.dot(attended, weight[...], preferred_element_type=F32).astype(BF)
    core = lax.axis_index("core")
    for pair in range(8):
        for which in range(2):
            target = pair * 2 + (core if which == 0 else 1 - core)
            for feature in range(2):
                at = (pair * 2 + feature) * C
                out[target, feature] = projected[which * 32 : which * 32 + 32, at : at + C]


def attend(queries, pairs, weight):
    return pl.pallas_call(
        attend_kernel,
        out_shape=pltpu.VMEM((16, 2, 32, C), BF),
        compiler_params=params(),
        name="attend",
    )(*near(queries, pairs, weight))


def unembed_kernel(mixed, own, other, out, values, rows):
    core = lax.axis_index("core")
    for which in range(2):
        feature = core if which == 0 else 1 - core
        for y in range(4):
            for r in range(8):
                at = pl.ds((which * 4 + y) * C, C)
                values[pl.ds(r * 32, 32), at] = mixed[r * 4 + y, feature]
    for pair in range(4):
        at = pl.ds(1024 + pair * 2 * C, 2 * C)
        wide = [weight[y, at] for weight in (own, other) for y in range(4)]
        result = lax.dot_general(
            values[...],
            jnp.concatenate(wide, axis=1),
            (((1,), (1,)), ((), ())),
            preferred_element_type=F32,
        )
        for j in range(2):
            column = result[:, j * C : j * C + C]
            rows[pl.ds(2 * pair + j, 256, stride=8), :] = column
    out[...] = rows[...].astype(BF).reshape(64, 32, C)


def unembed(mixed, own, other):
    return pl.pallas_call(
        unembed_kernel,
        out_shape=pltpu.VMEM((64, 32, C), BF),
        scratch_shapes=[
            pltpu.VMEM((256, 1024), BF),
            pltpu.VMEM((2048, C), F32),
        ],
        compiler_params=params(),
        name="unembed",
    )(*near(mixed, own, other))


def finish_kernel(features, received, out, patch, spread):
    frame, step = pl.program_id(0), pl.program_id(1)

    @pl.when((frame == 0) & (step == 0))
    def _():
        for r in range(8):
            for y in range(4):
                total = received[r * 8 + y].astype(F32) + received[r * 8 + 4 + y].astype(F32)
                patch[r * 4 + y] = total.astype(BF).astype(F32)

    token = frame * 2 + step
    at = pl.ds(pl.multiple_of(token * 8, 8), 8)
    for q in range(SPREAD // 4):
        piece = q * 2
        small = jnp.concatenate([patch[piece, at, :], patch[piece + 1, at, :]], axis=0)
        for row in range(4):
            for m in range(4):
                value = features[frame, step * SPREAD + q * 4 + row, m].astype(F32) + small
                spread[q * 4 + row, pl.ds(m, 16, stride=4), :] = value
    out[0] = spread[...].astype(BF)


def finish(features, received):
    return pl.pallas_call(
        finish_kernel,
        grid=(2, 128 // SPREAD),
        in_specs=[VMEM, VMEM],
        out_specs=pl.BlockSpec((1, SPREAD, 64, C), lambda f, i: (f, i, 0, 0)),
        out_shape=jax.ShapeDtypeStruct((2, 128, 64, C), BF),
        scratch_shapes=[
            pltpu.VMEM((32, 32, C), F32),
            pltpu.VMEM((SPREAD, 64, C), F32),
        ],
        compiler_params=params(),
        name="finish",
    )(*near(features, received))


def exchange(array, axes):
    return lax.all_to_all(array, axes, 0, 0, tiled=True)


def from_neighbours(low, high, axes, count):
    forward = [(i, i + 1) for i in range(count - 1)]
    backward = [(i + 1, i) for i in range(count - 1)]
    return lax.ppermute(low, axes, forward), lax.ppermute(high, axes, backward)


def on_device(frames, conv_weight, embed_weight, unembed_weight, qkv_weight, out_weight):
    left, right = from_neighbours(frames[:, :, 63], frames[:, :, 0], COL, 16)
    maps = [weight.reshape(4, 1024, C) for weight in (embed_weight, unembed_weight)]
    both = pack(*maps)
    left, right, both = lax.optimization_barrier((left, right, both))
    rows = [
        jnp.pad(
            jnp.concatenate([frames[:, y], left[:, y : y + 1], right[:, y : y + 1]], axis=1),
            ((0, 0), (0, 14), (0, 0)),
        )
        for y in (127, 0)
    ]
    top, bottom = from_neighbours(rows[0], rows[1], ROW, 8)
    own = exchange(both, "y")
    features, patches = convolve(frames, top, bottom, left, right, conv_weight)
    own, patches = lax.optimization_barrier((own, patches))
    other = lax.ppermute(own, "core", SWAP)
    partial = embed(exchange(patches, SAME), own, other)
    copies, embedded = sum_and_copy(8, exchange(partial, ROWY))
    group = exchange(copies, PLANE)
    queries, pairs = project_qkv(group, lax.ppermute(group, "core", SWAP), qkv_weight)
    projected = attend(queries, exchange(pairs, ROW), out_weight)
    copies, _ = sum_and_copy(32, exchange(projected, COL), embedded)
    patch_values = unembed(exchange(copies, ROWY), own, other)
    return finish(features, exchange(patch_values, SAME))


def solution(mesh):
    fine = jax.sharding.Mesh(mesh.devices.reshape(4, 2, 2, 4, 2), EVERY)
    placed = (
        P(None, ROW, COL, None),
        P(),
        P(ROW, COL),
        P(ROW, COL),
        P(None, None, COL),
        P(COL, None),
    )
    return jax.shard_map(
        on_device,
        mesh=fine,
        in_specs=placed,
        out_specs=P(None, ROW, COL, None),
        check_vma=False,
    )
```

```python
import functools

import jax
import jax.numpy as jnp
from jax import lax
from jax.experimental import pallas as pl
from jax.experimental.pallas import tpu as pltpu
from jax.sharding import PartitionSpec as P

C = 128
BF = jnp.bfloat16
F32 = jnp.float32
EPS = 1e-06
ROW = ("z", "xl")
COL = ("xh", "y", "core")
ROWY = ("xl", "y", "z")
PLANE = ("xh", "y")
SAME = ("y", "xh", "xl", "z")
EVERY = ROW + COL
SWAP = [(0, 1), (1, 0)]
CHUNK = 64
SPREAD = 128
SUB = 16
LEFT = 8


def params(mib=12):
    return pltpu.CompilerParams(vmem_limit_bytes=mib * 2**20)


def in_rowy(r, y):
    return ((r % 2) * 4 + y) * 4 + r // 2


def in_same(r, xh, y):
    return ((y * 2 + xh) * 2 + r % 2) * 4 + r // 2


def near(*arrays):
    return [pltpu.with_memory_space_constraint(array, pltpu.VMEM) for array in arrays]


VMEM = pl.BlockSpec(memory_space=pltpu.VMEM)


def pack_kernel(first, second, both, held, arrived, left):
    pieces = [(i, y, part) for i, part in enumerate((first, second)) for y in range(4)]
    loads = [
        pltpu.make_async_copy(part.at[y], held.at[i, y], arrived.at[i, y])
        for i, y, part in pieces
    ]
    stores = [
        pltpu.make_async_copy(held.at[i, y], both.at[y, pl.ds(1024 * i, 1024)], left.at[i, y])
        for i, y, _ in pieces
    ]
    for copy in loads:
        copy.start()
    for load, store in zip(loads, stores):
        load.wait()
        store.start()
    for copy in stores:
        copy.wait()


def pack(first, second):
    hbm = pl.BlockSpec(memory_space=pltpu.HBM)
    return pl.pallas_call(
        pack_kernel,
        in_specs=[hbm] * 2,
        out_specs=hbm,
        out_shape=pltpu.HBM((4, 2048, C), BF),
        scratch_shapes=[
            pltpu.VMEM((2, 4, 1024, C), BF),
            pltpu.SemaphoreType.DMA((2, 4)),
            pltpu.SemaphoreType.DMA((2, 4)),
        ],
        compiler_params=params(),
        name="pack",
    )(*(pltpu.with_memory_space_constraint(a, pltpu.HBM) for a in (first, second)))


def conv_kernel(
    main, above, below, top, bottom, left, right, weight, features, send, padded, taps, kernel, pooled
):
    frame, step = pl.program_id(0), pl.program_id(1)

    @pl.when((frame == 0) & (step == 0))
    def _():
        for a in range(3):
            for k in range(4):
                for o in range(2):
                    b = k - o
                    block = weight[a, b] if 0 <= b <= 2 else jnp.zeros((C, C), BF)
                    kernel[pl.ds(a * 512 + k * C, C), pl.ds(o * C, C)] = block

    cols = pl.ds(LEFT, 64)
    start = step * CHUNK
    padded[pl.ds(1, CHUNK), cols, :] = main[0].astype(F32)
    rows = pl.ds(pl.multiple_of(start, CHUNK), CHUNK)
    padded[pl.ds(1, CHUNK), LEFT - 1, :] = left[frame, rows, :].astype(F32)
    padded[pl.ds(1, CHUNK), LEFT + 64, :] = right[frame, rows, :].astype(F32)
    for border, outside, inside, row, at in (
        (step == 0, top, above, CHUNK - 1, 0),
        (step == 1, bottom, below, CHUNK, CHUNK + 1),
    ):

        @pl.when(border)
        def _(outside=outside, at=at):
            padded[at, cols, :] = outside[frame, pl.ds(0, 64)].astype(F32)
            corners = outside[frame, pl.ds(64, 16)].astype(F32)
            padded[at, pl.ds(LEFT - 1, 1), :] = corners[:1]
            padded[at, pl.ds(LEFT + 64, 1), :] = corners[1:2]

        @pl.when(jnp.logical_not(border))
        def _(inside=inside, row=row, at=at):
            padded[at, cols, :] = inside[0, 0].astype(F32)
            near_row = pl.ds(row // 16 * 16, 16)
            for side, col in ((left, LEFT - 1), (right, LEFT + 64)):
                value = side[frame, near_row, :].astype(F32)
                padded[at, pl.ds(col, 1), :] = value[row % 16 : row % 16 + 1]

    for k in range(6):
        taps[:, :, pl.ds(k * C, C)] = padded[:, pl.ds(LEFT - 1 + k, 16, stride=4), :].astype(BF)

    for sub in range(CHUNK // SUB):
        total = jnp.zeros((SUB // 4, 16, C), F32)
        for pair in range(2):
            lhs = jnp.concatenate(
                [
                    taps[pl.ds(sub * SUB + a, SUB), :, pl.ds(pair * 256, 512)].reshape(SUB * 16, 512)
                    for a in range(3)
                ],
                axis=1,
            )
            result = jnp.dot(lhs, kernel[...], preferred_element_type=F32)
            for o in range(2):
                m = pair * 2 + o
                v = result[:, o * C : (o + 1) * C]
                mean = jnp.mean(v * v, axis=-1, keepdims=True)
                h = v * (0.5 * lax.rsqrt(mean + EPS))
                x = taps[pl.ds(sub * SUB + 1, SUB), :, pl.ds((m + 1) * C, C)].reshape(SUB * 16, C)
                f = x.astype(F32) + (h + h * jnp.tanh(h))
                f = f.reshape(SUB, 16, C)
                features[0, pl.ds(sub * SUB, SUB), m] = f.astype(BF)
                total = total + f.reshape(SUB // 4, 4, 16, C).sum(axis=1)
        mean = total * (1.0 / 16.0)
        for g in range(SUB // 4):
            q = sub * (SUB // 4) + g
            token = frame * 2 + step
            for half in range(2):
                piece = q * 2 + half
                at = pl.ds(pl.multiple_of(token * 8, 8), 8)
                pooled[piece, at, :] = mean[g, half * 8 : half * 8 + 8]

    @pl.when((frame == 1) & (step == 1))
    def _():
        for r in range(8):
            for y in range(4):
                block = pooled[r * 4 + y].astype(BF)
                for xh in range(2):
                    send[in_same(r, xh, y)] = block


def convolve(frames, top, bottom, left, right, weight):
    steps = 128 // CHUNK
    far = pltpu.with_memory_space_constraint(frames, pltpu.HBM)
    return pl.pallas_call(
        conv_kernel,
        grid=(2, steps),
        in_specs=[
            pl.BlockSpec((1, CHUNK, 64, C), lambda f, i: (f, i, 0, 0)),
            pl.BlockSpec((1, 1, 64, C), lambda f, i: (f, CHUNK - 1, 0, 0)),
            pl.BlockSpec((1, 1, 64, C), lambda f, i: (f, CHUNK, 0, 0)),
        ]
        + [VMEM] * 5,
        out_specs=[pl.BlockSpec((1, CHUNK, 4, 16, C), lambda f, i: (f, i, 0, 0, 0)), VMEM],
        out_shape=[
            pltpu.HBM((2, 128, 4, 16, C), BF),
            pltpu.VMEM((64, 32, C), BF),
        ],
        scratch_shapes=[
            pltpu.VMEM((CHUNK + 2, 80, C), F32),
            pltpu.VMEM((CHUNK + 2, 16, 6 * C), BF),
            pltpu.VMEM((3 * 512, 2 * C), BF),
            pltpu.VMEM((32, 32, C), F32),
        ],
        compiler_params=params(),
        cost_estimate=pl.CostEstimate(
            flops=2 * 16384 * 9 * C * C, bytes_accessed=9 * 2**20, transcendentals=2 * 16384 * C
        ),
        name="conv_block",
    )(far, far, far, *near(top, bottom, left, right, weight))


def embed_kernel(received, own, other, out, rows, values):
    core = lax.axis_index("core")
    for r in range(8):
        for xh in range(2):
            for y in range(4):
                at = pl.ds(((r * 2 + xh) * 4 + y) * 32, 32)
                rows[at, :] = received[in_same(r, xh, y)].astype(F32)
    for j in range(8):
        values[:, pl.ds(j * C, C)] = rows[pl.ds(j, 256, stride=8), :].astype(BF)
    for which, weight in enumerate((own, other)):
        wide = jnp.concatenate([weight[y, pl.ds(0, 1024)] for y in range(4)], axis=1)
        result = jnp.dot(values[...], wide, preferred_element_type=F32).astype(BF)
        feature = core if which == 0 else 1 - core
        for r in range(8):
            for y in range(4):
                out[in_rowy(r, y), feature] = result[r * 32 : r * 32 + 32, y * C : y * C + C]


def embed(received, own, other):
    return pl.pallas_call(
        embed_kernel,
        out_shape=pltpu.VMEM((32, 2, 32, C), BF),
        scratch_shapes=[
            pltpu.VMEM((2048, C), F32),
            pltpu.VMEM((256, 1024), BF),
        ],
        compiler_params=params(),
        name="embed",
    )(*near(received, own, other))


def sum_kernel(copies, terms, *rest):
    out, total_out = rest[-2:]
    total = terms[0].astype(F32)
    for i in range(1, terms.shape[0]):
        total = total + terms[i].astype(F32)
    if len(rest) == 3:
        total = rest[0][...].astype(F32) + total
    total = total.astype(BF)
    total_out[...] = total
    for i in range(copies):
        out[i] = total


def sum_and_copy(copies, terms, *base):
    return pl.pallas_call(
        functools.partial(sum_kernel, copies),
        out_shape=[pltpu.VMEM((copies, 2, 32, C), BF), pltpu.VMEM((2, 32, C), BF)],
        compiler_params=params(),
        name="sum_and_copy",
    )(*near(terms, *base))


def qkv_kernel(own, other, weight, queries, pairs):
    normed = []
    for group in (own, other):
        blocks = [group[pair, feature].astype(F32) for pair in range(8) for feature in range(2)]
        square = sum(block * block for block in blocks)
        square = jnp.sum(square, axis=-1, keepdims=True)
        scale = lax.rsqrt(square * (1.0 / 2048.0) + EPS)
        normed.append(jnp.concatenate([(block * scale).astype(BF) for block in blocks], axis=1))
    normed = jnp.concatenate(normed, axis=0)
    queries[...] = jnp.dot(normed, weight[0], preferred_element_type=F32).astype(BF)
    for part in range(2):
        result = jnp.dot(normed, weight[1 + part], preferred_element_type=F32).astype(BF)
        for r in range(8):
            pairs[r, part] = result


def project_qkv(own, other, weight):
    return pl.pallas_call(
        qkv_kernel,
        out_shape=[pltpu.VMEM((64, C), BF), pltpu.VMEM((8, 2, 64, C), BF)],
        compiler_params=params(),
        name="qkv",
    )(*near(own, other, weight))


def attend_kernel(queries, pairs, weight, out):
    keys = pairs[:, 0].reshape(512, C)
    values = pairs[:, 1].reshape(512, C)
    scores = lax.dot_general(
        queries[...], keys, (((1,), (1,)), ((), ())), preferred_element_type=F32
    ) * C ** (-0.5)
    scores = jnp.exp(scores - jnp.max(scores, axis=-1, keepdims=True))
    weights = (scores / jnp.sum(scores, axis=-1, keepdims=True)).astype(BF)
    attended = jnp.dot(weights, values, preferred_element_type=F32).astype(BF)
    projected = jnp.dot(attended, weight[...], preferred_element_type=F32).astype(BF)
    core = lax.axis_index("core")
    for pair in range(8):
        for which in range(2):
            target = pair * 2 + (core if which == 0 else 1 - core)
            for feature in range(2):
                at = (pair * 2 + feature) * C
                out[target, feature] = projected[which * 32 : which * 32 + 32, at : at + C]


def attend(queries, pairs, weight):
    return pl.pallas_call(
        attend_kernel,
        out_shape=pltpu.VMEM((16, 2, 32, C), BF),
        compiler_params=params(),
        name="attend",
    )(*near(queries, pairs, weight))


def unembed_kernel(mixed, own, other, out, values, rows):
    core = lax.axis_index("core")
    for which in range(2):
        feature = core if which == 0 else 1 - core
        for y in range(4):
            for r in range(8):
                at = pl.ds((which * 4 + y) * C, C)
                values[pl.ds(r * 32, 32), at] = mixed[in_rowy(r, y), feature]
    for pair in range(4):
        at = pl.ds(1024 + pair * 2 * C, 2 * C)
        wide = [weight[y, at] for weight in (own, other) for y in range(4)]
        result = lax.dot_general(
            values[...],
            jnp.concatenate(wide, axis=1),
            (((1,), (1,)), ((), ())),
            preferred_element_type=F32,
        )
        for j in range(2):
            column = result[:, j * C : j * C + C]
            rows[pl.ds(2 * pair + j, 256, stride=8), :] = column
    for r in range(8):
        for xh in range(2):
            for y in range(4):
                at = pl.ds(((r * 2 + xh) * 4 + y) * 32, 32)
                out[in_same(r, xh, y)] = rows[at, :].astype(BF)


def unembed(mixed, own, other):
    return pl.pallas_call(
        unembed_kernel,
        out_shape=pltpu.VMEM((64, 32, C), BF),
        scratch_shapes=[
            pltpu.VMEM((256, 1024), BF),
            pltpu.VMEM((2048, C), F32),
        ],
        compiler_params=params(),
        name="unembed",
    )(*near(mixed, own, other))


def finish_kernel(features, received, out, patch, spread):
    frame, step = pl.program_id(0), pl.program_id(1)

    @pl.when((frame == 0) & (step == 0))
    def _():
        for r in range(8):
            for y in range(4):
                first, second = (received[in_same(r, xh, y)].astype(F32) for xh in range(2))
                total = first + second
                patch[r * 4 + y] = total.astype(BF).astype(F32)

    for q in range(SPREAD // 4):
        token = frame * 2 + q // 16
        at = pl.ds(pl.multiple_of(token * 8, 8), 8)
        piece = q % 16 * 2
        small = jnp.concatenate([patch[piece, at, :], patch[piece + 1, at, :]], axis=0)
        for row in range(4):
            for m in range(4):
                value = features[frame, step * SPREAD + q * 4 + row, m].astype(F32) + small
                spread[q * 4 + row, pl.ds(m, 16, stride=4), :] = value
    out[0] = spread[...].astype(BF)


def finish(features, received):
    return pl.pallas_call(
        finish_kernel,
        grid=(2, 128 // SPREAD),
        in_specs=[VMEM, VMEM],
        out_specs=pl.BlockSpec((1, SPREAD, 64, C), lambda f, i: (f, i, 0, 0)),
        out_shape=jax.ShapeDtypeStruct((2, 128, 64, C), BF),
        scratch_shapes=[
            pltpu.VMEM((32, 32, C), F32),
            pltpu.VMEM((SPREAD, 64, C), F32),
        ],
        compiler_params=params(),
        name="finish",
    )(*near(features, received))


def exchange(array, axes):
    return lax.all_to_all(array, axes, 0, 0, tiled=True)


def from_neighbours(low, high, axes, count):
    forward = [(i, i + 1) for i in range(count - 1)]
    backward = [(i + 1, i) for i in range(count - 1)]
    return lax.ppermute(low, axes, forward), lax.ppermute(high, axes, backward)


def on_device(frames, conv_weight, embed_weight, unembed_weight, qkv_weight, out_weight):
    left, right = from_neighbours(frames[:, :, 63], frames[:, :, 0], COL, 16)
    maps = [weight.reshape(4, 1024, C) for weight in (embed_weight, unembed_weight)]
    both = pack(*maps)
    left, right, both = lax.optimization_barrier((left, right, both))
    rows = [
        jnp.pad(
            jnp.concatenate([frames[:, y], left[:, y : y + 1], right[:, y : y + 1]], axis=1),
            ((0, 0), (0, 14), (0, 0)),
        )
        for y in (127, 0)
    ]
    top, bottom = from_neighbours(rows[0], rows[1], ROW, 8)
    own = exchange(both, "y")
    features, patches = convolve(frames, top, bottom, left, right, conv_weight)
    own, patches = lax.optimization_barrier((own, patches))
    other = lax.ppermute(own, "core", SWAP)
    partial = embed(exchange(patches, SAME), own, other)
    copies, embedded = sum_and_copy(8, exchange(partial, ROWY))
    group = exchange(copies, PLANE)
    queries, pairs = project_qkv(group, lax.ppermute(group, "core", SWAP), qkv_weight)
    projected = attend(queries, exchange(pairs, ROW), out_weight)
    copies, _ = sum_and_copy(32, exchange(projected, COL), embedded)
    patch_values = unembed(exchange(copies, ROWY), own, other)
    return finish(features, exchange(patch_values, SAME))


def solution(mesh):
    fine = jax.sharding.Mesh(mesh.devices.reshape(4, 2, 2, 4, 2), EVERY)
    placed = (
        P(None, ROW, COL, None),
        P(),
        P(ROW, COL),
        P(ROW, COL),
        P(None, None, COL),
        P(COL, None),
    )
    return jax.shard_map(
        on_device,
        mesh=fine,
        in_specs=placed,
        out_specs=P(None, ROW, COL, None),
        check_vma=False,
    )
```

```python
import functools

import jax
import jax.numpy as jnp
from jax import lax
from jax.experimental import pallas as pl
from jax.experimental.pallas import tpu as pltpu
from jax.sharding import PartitionSpec as P

C = 128
BF = jnp.bfloat16
F32 = jnp.float32
EPS = 1e-06
ROW = ("z", "xl")
COL = ("xh", "y", "core")
ACROSS = ("core", "y", "xh")
ROWY = ("xl", "y", "z")
SAME = ("y", "xh", "xl", "z")
EVERY = ROW + COL
SWAP = [(0, 1), (1, 0)]
CHUNK = 64
SPREAD = 128
SUB = 16
LEFT = 8


def params(mib=12):
    return pltpu.CompilerParams(vmem_limit_bytes=mib * 2**20)


def in_rowy(r, y):
    return ((r % 2) * 4 + y) * 4 + r // 2


def in_same(r, xh, y):
    return ((y * 2 + xh) * 2 + r % 2) * 4 + r // 2


def near(*arrays):
    return [pltpu.with_memory_space_constraint(array, pltpu.VMEM) for array in arrays]


VMEM = pl.BlockSpec(memory_space=pltpu.VMEM)


def pack_kernel(first, second, both, held, arrived, left):
    pieces = [(i, y, part) for i, part in enumerate((first, second)) for y in range(4)]
    loads = [
        pltpu.make_async_copy(part.at[y], held.at[i, y], arrived.at[i, y])
        for i, y, part in pieces
    ]
    stores = [
        pltpu.make_async_copy(held.at[i, y], both.at[y, pl.ds(1024 * i, 1024)], left.at[i, y])
        for i, y, _ in pieces
    ]
    for copy in loads:
        copy.start()
    for load, store in zip(loads, stores):
        load.wait()
        store.start()
    for copy in stores:
        copy.wait()


def pack(first, second):
    hbm = pl.BlockSpec(memory_space=pltpu.HBM)
    return pl.pallas_call(
        pack_kernel,
        in_specs=[hbm] * 2,
        out_specs=hbm,
        out_shape=pltpu.HBM((4, 2048, C), BF),
        scratch_shapes=[
            pltpu.VMEM((2, 4, 1024, C), BF),
            pltpu.SemaphoreType.DMA((2, 4)),
            pltpu.SemaphoreType.DMA((2, 4)),
        ],
        compiler_params=params(),
        name="pack",
    )(*(pltpu.with_memory_space_constraint(a, pltpu.HBM) for a in (first, second)))


def conv_kernel(
    main, above, below, top, bottom, left, right, weight, features, send, padded, taps, kernel, pooled
):
    frame, step = pl.program_id(0), pl.program_id(1)

    @pl.when((frame == 0) & (step == 0))
    def _():
        for a in range(3):
            for k in range(4):
                for o in range(2):
                    b = k - o
                    block = weight[a, b] if 0 <= b <= 2 else jnp.zeros((C, C), BF)
                    kernel[pl.ds(a * 512 + k * C, C), pl.ds(o * C, C)] = block

    cols = pl.ds(LEFT, 64)
    start = step * CHUNK
    padded[pl.ds(1, CHUNK), cols, :] = main[0].astype(F32)
    rows = pl.ds(pl.multiple_of(start, CHUNK), CHUNK)
    padded[pl.ds(1, CHUNK), LEFT - 1, :] = left[frame, rows, :].astype(F32)
    padded[pl.ds(1, CHUNK), LEFT + 64, :] = right[frame, rows, :].astype(F32)
    for border, outside, inside, row, at in (
        (step == 0, top, above, CHUNK - 1, 0),
        (step == 1, bottom, below, CHUNK, CHUNK + 1),
    ):

        @pl.when(border)
        def _(outside=outside, at=at):
            padded[at, cols, :] = outside[frame, pl.ds(0, 64)].astype(F32)
            corners = outside[frame, pl.ds(64, 16)].astype(F32)
            padded[at, pl.ds(LEFT - 1, 1), :] = corners[:1]
            padded[at, pl.ds(LEFT + 64, 1), :] = corners[1:2]

        @pl.when(jnp.logical_not(border))
        def _(inside=inside, row=row, at=at):
            padded[at, cols, :] = inside[0, 0].astype(F32)
            near_row = pl.ds(row // 16 * 16, 16)
            for side, col in ((left, LEFT - 1), (right, LEFT + 64)):
                value = side[frame, near_row, :].astype(F32)
                padded[at, pl.ds(col, 1), :] = value[row % 16 : row % 16 + 1]

    for k in range(6):
        taps[:, :, pl.ds(k * C, C)] = padded[:, pl.ds(LEFT - 1 + k, 16, stride=4), :].astype(BF)

    for sub in range(CHUNK // SUB):
        total = jnp.zeros((SUB // 4, 16, C), F32)
        for pair in range(2):
            lhs = jnp.concatenate(
                [
                    taps[pl.ds(sub * SUB + a, SUB), :, pl.ds(pair * 256, 512)].reshape(SUB * 16, 512)
                    for a in range(3)
                ],
                axis=1,
            )
            result = jnp.dot(lhs, kernel[...], preferred_element_type=F32)
            for o in range(2):
                m = pair * 2 + o
                v = result[:, o * C : (o + 1) * C]
                mean = jnp.mean(v * v, axis=-1, keepdims=True)
                h = v * (0.5 * lax.rsqrt(mean + EPS))
                x = taps[pl.ds(sub * SUB + 1, SUB), :, pl.ds((m + 1) * C, C)].reshape(SUB * 16, C)
                f = x.astype(F32) + (h + h * jnp.tanh(h))
                f = f.reshape(SUB, 16, C)
                features[0, pl.ds(sub * SUB, SUB), m] = f.astype(BF)
                total = total + f.reshape(SUB // 4, 4, 16, C).sum(axis=1)
        mean = total * (1.0 / 16.0)
        for g in range(SUB // 4):
            q = sub * (SUB // 4) + g
            token = frame * 2 + step
            for half in range(2):
                piece = q * 2 + half
                at = pl.ds(pl.multiple_of(token * 8, 8), 8)
                pooled[piece, at, :] = mean[g, half * 8 : half * 8 + 8]

    @pl.when((frame == 1) & (step == 1))
    def _():
        for r in range(8):
            for y in range(4):
                block = pooled[r * 4 + y].astype(BF)
                for xh in range(2):
                    send[in_same(r, xh, y)] = block


def convolve(frames, top, bottom, left, right, weight):
    steps = 128 // CHUNK
    far = pltpu.with_memory_space_constraint(frames, pltpu.HBM)
    return pl.pallas_call(
        conv_kernel,
        grid=(2, steps),
        in_specs=[
            pl.BlockSpec((1, CHUNK, 64, C), lambda f, i: (f, i, 0, 0)),
            pl.BlockSpec((1, 1, 64, C), lambda f, i: (f, CHUNK - 1, 0, 0)),
            pl.BlockSpec((1, 1, 64, C), lambda f, i: (f, CHUNK, 0, 0)),
        ]
        + [VMEM] * 5,
        out_specs=[pl.BlockSpec((1, CHUNK, 4, 16, C), lambda f, i: (f, i, 0, 0, 0)), VMEM],
        out_shape=[
            pltpu.HBM((2, 128, 4, 16, C), BF),
            pltpu.VMEM((64, 32, C), BF),
        ],
        scratch_shapes=[
            pltpu.VMEM((CHUNK + 2, 80, C), F32),
            pltpu.VMEM((CHUNK + 2, 16, 6 * C), BF),
            pltpu.VMEM((3 * 512, 2 * C), BF),
            pltpu.VMEM((32, 32, C), F32),
        ],
        compiler_params=params(),
        cost_estimate=pl.CostEstimate(
            flops=2 * 16384 * 9 * C * C, bytes_accessed=9 * 2**20, transcendentals=2 * 16384 * C
        ),
        name="conv_block",
    )(far, far, far, *near(top, bottom, left, right, weight))


def embed_kernel(received, own, other, out, rows, values):
    core = lax.axis_index("core")
    for r in range(8):
        for xh in range(2):
            for y in range(4):
                at = pl.ds(((r * 2 + xh) * 4 + y) * 32, 32)
                rows[at, :] = received[in_same(r, xh, y)].astype(F32)
    for j in range(8):
        values[:, pl.ds(j * C, C)] = rows[pl.ds(j, 256, stride=8), :].astype(BF)
    for which, weight in enumerate((own, other)):
        wide = jnp.concatenate([weight[y, pl.ds(0, 1024)] for y in range(4)], axis=1)
        result = jnp.dot(values[...], wide, preferred_element_type=F32).astype(BF)
        feature = core if which == 0 else 1 - core
        for r in range(8):
            for y in range(4):
                out[in_rowy(r, y), feature] = result[r * 32 : r * 32 + 32, y * C : y * C + C]


def embed(received, own, other):
    return pl.pallas_call(
        embed_kernel,
        out_shape=pltpu.VMEM((32, 2, 32, C), BF),
        scratch_shapes=[
            pltpu.VMEM((2048, C), F32),
            pltpu.VMEM((256, 1024), BF),
        ],
        compiler_params=params(),
        name="embed",
    )(*near(received, own, other))


def sum_kernel(copies, terms, *rest):
    out, total_out = rest[-2:]
    total = terms[0].astype(F32)
    for i in range(1, terms.shape[0]):
        total = total + terms[i].astype(F32)
    if len(rest) == 3:
        total = rest[0][...].astype(F32) + total
    total = total.astype(BF)
    total_out[...] = total
    for i in range(copies):
        out[i] = total


def sum_and_copy(copies, terms, *base):
    return pl.pallas_call(
        functools.partial(sum_kernel, copies),
        out_shape=[pltpu.VMEM((copies, 2, 32, C), BF), pltpu.VMEM((2, 32, C), BF)],
        compiler_params=params(),
        name="sum_and_copy",
    )(*near(terms, *base))


def qkv_kernel(embedded, weight, queries, pairs):
    normed = []
    for core in range(2):
        blocks = [
            embedded[core * 8 + pair % 4 * 2 + pair // 4, feature].astype(F32)
            for pair in range(8)
            for feature in range(2)
        ]
        square = sum(block * block for block in blocks)
        square = jnp.sum(square, axis=-1, keepdims=True)
        scale = lax.rsqrt(square * (1.0 / 2048.0) + EPS)
        normed.append(jnp.concatenate([(block * scale).astype(BF) for block in blocks], axis=1))
    normed = jnp.concatenate(normed, axis=0)
    queries[...] = jnp.dot(normed, weight[0], preferred_element_type=F32).astype(BF)
    for part in range(2):
        result = jnp.dot(normed, weight[1 + part], preferred_element_type=F32).astype(BF)
        for r in range(8):
            pairs[r, part] = result


def project_qkv(embedded, weight):
    return pl.pallas_call(
        qkv_kernel,
        out_shape=[pltpu.VMEM((64, C), BF), pltpu.VMEM((8, 2, 64, C), BF)],
        compiler_params=params(),
        name="qkv",
    )(*near(embedded, weight))


def attend_kernel(queries, pairs, weight, out):
    keys = pairs[:, 0].reshape(512, C)
    values = pairs[:, 1].reshape(512, C)
    scores = lax.dot_general(
        queries[...], keys, (((1,), (1,)), ((), ())), preferred_element_type=F32
    ) * C ** (-0.5)
    scores = jnp.exp(scores - jnp.max(scores, axis=-1, keepdims=True))
    weights = (scores / jnp.sum(scores, axis=-1, keepdims=True)).astype(BF)
    attended = jnp.dot(weights, values, preferred_element_type=F32).astype(BF)
    projected = jnp.dot(attended, weight[...], preferred_element_type=F32).astype(BF)
    for pair in range(8):
        for which in range(2):
            target = which * 8 + pair % 4 * 2 + pair // 4
            for feature in range(2):
                at = (pair * 2 + feature) * C
                out[target, feature] = projected[which * 32 : which * 32 + 32, at : at + C]


def attend(queries, pairs, weight):
    return pl.pallas_call(
        attend_kernel,
        out_shape=pltpu.VMEM((16, 2, 32, C), BF),
        compiler_params=params(),
        name="attend",
    )(*near(queries, pairs, weight))


def unembed_kernel(mixed, own, other, out, values, rows):
    core = lax.axis_index("core")
    for which in range(2):
        feature = core if which == 0 else 1 - core
        for y in range(4):
            for r in range(8):
                at = pl.ds((which * 4 + y) * C, C)
                values[pl.ds(r * 32, 32), at] = mixed[in_rowy(r, y), feature]
    for pair in range(4):
        at = pl.ds(1024 + pair * 2 * C, 2 * C)
        wide = [weight[y, at] for weight in (own, other) for y in range(4)]
        result = lax.dot_general(
            values[...],
            jnp.concatenate(wide, axis=1),
            (((1,), (1,)), ((), ())),
            preferred_element_type=F32,
        )
        for j in range(2):
            column = result[:, j * C : j * C + C]
            rows[pl.ds(2 * pair + j, 256, stride=8), :] = column
    for r in range(8):
        for xh in range(2):
            for y in range(4):
                at = pl.ds(((r * 2 + xh) * 4 + y) * 32, 32)
                out[in_same(r, xh, y)] = rows[at, :].astype(BF)


def unembed(mixed, own, other):
    return pl.pallas_call(
        unembed_kernel,
        out_shape=pltpu.VMEM((64, 32, C), BF),
        scratch_shapes=[
            pltpu.VMEM((256, 1024), BF),
            pltpu.VMEM((2048, C), F32),
        ],
        compiler_params=params(),
        name="unembed",
    )(*near(mixed, own, other))


def finish_kernel(features, received, out, patch, spread):
    frame, step = pl.program_id(0), pl.program_id(1)

    @pl.when((frame == 0) & (step == 0))
    def _():
        for r in range(8):
            for y in range(4):
                first, second = (received[in_same(r, xh, y)].astype(F32) for xh in range(2))
                total = first + second
                patch[r * 4 + y] = total.astype(BF).astype(F32)

    for q in range(SPREAD // 4):
        token = frame * 2 + q // 16
        at = pl.ds(pl.multiple_of(token * 8, 8), 8)
        piece = q % 16 * 2
        small = jnp.concatenate([patch[piece, at, :], patch[piece + 1, at, :]], axis=0)
        for row in range(4):
            for m in range(4):
                value = features[frame, step * SPREAD + q * 4 + row, m].astype(F32) + small
                spread[q * 4 + row, pl.ds(m, 16, stride=4), :] = value
    out[0] = spread[...].astype(BF)


def finish(features, received):
    return pl.pallas_call(
        finish_kernel,
        grid=(2, 128 // SPREAD),
        in_specs=[VMEM, VMEM],
        out_specs=pl.BlockSpec((1, SPREAD, 64, C), lambda f, i: (f, i, 0, 0)),
        out_shape=jax.ShapeDtypeStruct((2, 128, 64, C), BF),
        scratch_shapes=[
            pltpu.VMEM((32, 32, C), F32),
            pltpu.VMEM((SPREAD, 64, C), F32),
        ],
        compiler_params=params(),
        name="finish",
    )(*near(features, received))


def exchange(array, axes):
    return lax.all_to_all(array, axes, 0, 0, tiled=True)


def from_neighbours(low, high, axes, count):
    forward = [(i, i + 1) for i in range(count - 1)]
    backward = [(i + 1, i) for i in range(count - 1)]
    return lax.ppermute(low, axes, forward), lax.ppermute(high, axes, backward)


def on_device(frames, conv_weight, embed_weight, unembed_weight, qkv_weight, out_weight):
    left, right = from_neighbours(frames[:, :, 63], frames[:, :, 0], COL, 16)
    maps = [weight.reshape(4, 1024, C) for weight in (embed_weight, unembed_weight)]
    both = pack(*maps)
    left, right, both = lax.optimization_barrier((left, right, both))
    rows = [
        jnp.pad(
            jnp.concatenate([frames[:, y], left[:, y : y + 1], right[:, y : y + 1]], axis=1),
            ((0, 0), (0, 14), (0, 0)),
        )
        for y in (127, 0)
    ]
    top, bottom = from_neighbours(rows[0], rows[1], ROW, 8)
    own = exchange(both, "y")
    features, patches = convolve(frames, top, bottom, left, right, conv_weight)
    own, patches = lax.optimization_barrier((own, patches))
    other = lax.ppermute(own, "core", SWAP)
    partial = embed(exchange(patches, SAME), own, other)
    copies, embedded = sum_and_copy(16, exchange(partial, ROWY))
    queries, pairs = project_qkv(exchange(copies, ACROSS), qkv_weight)
    projected = attend(queries, exchange(pairs, ROW), out_weight)
    copies, _ = sum_and_copy(32, exchange(projected, ACROSS), embedded)
    patch_values = unembed(exchange(copies, ROWY), own, other)
    return finish(features, exchange(patch_values, SAME))


def solution(mesh):
    fine = jax.sharding.Mesh(mesh.devices.reshape(4, 2, 2, 4, 2), EVERY)
    placed = (
        P(None, ROW, COL, None),
        P(),
        P(ROW, COL),
        P(ROW, COL),
        P(None, None, COL),
        P(COL, None),
    )
    return jax.shard_map(
        on_device,
        mesh=fine,
        in_specs=placed,
        out_specs=P(None, ROW, COL, None),
        check_vma=False,
    )
```

```python
import functools

import jax
import jax.numpy as jnp
from jax import lax
from jax.experimental import pallas as pl
from jax.experimental.pallas import tpu as pltpu
from jax.sharding import PartitionSpec as P

C = 128
BF = jnp.bfloat16
F32 = jnp.float32
EPS = 1e-06
ROW = ("z", "xl")
COL = ("xh", "y", "core")
ACROSS = ("core", "y", "xh")
ROWY = ("xl", "y", "z")
SAME = ("y", "xh", "xl", "z")
EVERY = ROW + COL
SWAP = [(0, 1), (1, 0)]
CHUNK = 64
SPREAD = 128
SUB = 8
LEFT = 8


def params(mib=12):
    return pltpu.CompilerParams(vmem_limit_bytes=mib * 2**20)


def in_rowy(r, y):
    return ((r % 2) * 4 + y) * 4 + r // 2


def in_same(r, xh, y):
    return ((y * 2 + xh) * 2 + r % 2) * 4 + r // 2


def near(*arrays):
    return [pltpu.with_memory_space_constraint(array, pltpu.VMEM) for array in arrays]


VMEM = pl.BlockSpec(memory_space=pltpu.VMEM)


def pack_kernel(first, second, both, held, arrived, left):
    pieces = [(i, y, part) for i, part in enumerate((first, second)) for y in range(4)]
    loads = [
        pltpu.make_async_copy(part.at[y], held.at[i, y], arrived.at[i, y])
        for i, y, part in pieces
    ]
    stores = [
        pltpu.make_async_copy(held.at[i, y], both.at[y, pl.ds(1024 * i, 1024)], left.at[i, y])
        for i, y, _ in pieces
    ]
    for copy in loads:
        copy.start()
    for load, store in zip(loads, stores):
        load.wait()
        store.start()
    for copy in stores:
        copy.wait()


def pack(first, second):
    hbm = pl.BlockSpec(memory_space=pltpu.HBM)
    return pl.pallas_call(
        pack_kernel,
        in_specs=[hbm] * 2,
        out_specs=hbm,
        out_shape=pltpu.HBM((4, 2048, C), BF),
        scratch_shapes=[
            pltpu.VMEM((2, 4, 1024, C), BF),
            pltpu.SemaphoreType.DMA((2, 4)),
            pltpu.SemaphoreType.DMA((2, 4)),
        ],
        compiler_params=params(),
        name="pack",
    )(*(pltpu.with_memory_space_constraint(a, pltpu.HBM) for a in (first, second)))


def conv_kernel(
    main, above, below, top, bottom, left, right, weight, features, send, padded, taps, kernel, pooled
):
    frame, step = pl.program_id(0), pl.program_id(1)

    @pl.when((frame == 0) & (step == 0))
    def _():
        for a in range(3):
            for k in range(4):
                for o in range(2):
                    b = k - o
                    block = weight[a, b] if 0 <= b <= 2 else jnp.zeros((C, C), BF)
                    kernel[pl.ds(a * 512 + k * C, C), pl.ds(o * C, C)] = block

    cols = pl.ds(LEFT, 64)
    start = step * CHUNK
    padded[pl.ds(1, CHUNK), cols, :] = main[0].astype(F32)
    rows = pl.ds(pl.multiple_of(start, CHUNK), CHUNK)
    padded[pl.ds(1, CHUNK), LEFT - 1, :] = left[frame, rows, :].astype(F32)
    padded[pl.ds(1, CHUNK), LEFT + 64, :] = right[frame, rows, :].astype(F32)
    for border, outside, inside, row, at in (
        (step == 0, top, above, CHUNK - 1, 0),
        (step == 1, bottom, below, CHUNK, CHUNK + 1),
    ):

        @pl.when(border)
        def _(outside=outside, at=at):
            padded[at, cols, :] = outside[frame, pl.ds(0, 64)].astype(F32)
            corners = outside[frame, pl.ds(64, 16)].astype(F32)
            padded[at, pl.ds(LEFT - 1, 1), :] = corners[:1]
            padded[at, pl.ds(LEFT + 64, 1), :] = corners[1:2]

        @pl.when(jnp.logical_not(border))
        def _(inside=inside, row=row, at=at):
            padded[at, cols, :] = inside[0, 0].astype(F32)
            near_row = pl.ds(row // 16 * 16, 16)
            for side, col in ((left, LEFT - 1), (right, LEFT + 64)):
                value = side[frame, near_row, :].astype(F32)
                padded[at, pl.ds(col, 1), :] = value[row % 16 : row % 16 + 1]

    for k in range(6):
        taps[:, :, pl.ds(k * C, C)] = padded[:, pl.ds(LEFT - 1 + k, 16, stride=4), :].astype(BF)

    for sub in range(CHUNK // SUB):
        total = jnp.zeros((SUB // 4, 16, C), F32)
        for pair in range(2):
            lhs = jnp.concatenate(
                [
                    taps[pl.ds(sub * SUB + a, SUB), :, pl.ds(pair * 256, 512)].reshape(SUB * 16, 512)
                    for a in range(3)
                ],
                axis=1,
            )
            result = jnp.dot(lhs, kernel[...], preferred_element_type=F32)
            for o in range(2):
                m = pair * 2 + o
                v = result[:, o * C : (o + 1) * C]
                mean = jnp.mean(v * v, axis=-1, keepdims=True)
                h = v * (0.5 * lax.rsqrt(mean + EPS))
                x = taps[pl.ds(sub * SUB + 1, SUB), :, pl.ds((m + 1) * C, C)].reshape(SUB * 16, C)
                f = x.astype(F32) + (h + h * jnp.tanh(h))
                f = f.reshape(SUB, 16, C)
                features[0, pl.ds(sub * SUB, SUB), m] = f.astype(BF)
                total = total + f.reshape(SUB // 4, 4, 16, C).sum(axis=1)
        mean = total * (1.0 / 16.0)
        for g in range(SUB // 4):
            q = sub * (SUB // 4) + g
            token = frame * 2 + step
            for half in range(2):
                piece = q * 2 + half
                at = pl.ds(pl.multiple_of(token * 8, 8), 8)
                pooled[piece, at, :] = mean[g, half * 8 : half * 8 + 8]

    @pl.when((frame == 1) & (step == 1))
    def _():
        for r in range(8):
            for y in range(4):
                block = pooled[r * 4 + y].astype(BF)
                for xh in range(2):
                    send[in_same(r, xh, y)] = block


def convolve(frames, top, bottom, left, right, weight):
    steps = 128 // CHUNK
    far = pltpu.with_memory_space_constraint(frames, pltpu.HBM)
    return pl.pallas_call(
        conv_kernel,
        grid=(2, steps),
        in_specs=[
            pl.BlockSpec((1, CHUNK, 64, C), lambda f, i: (f, i, 0, 0)),
            pl.BlockSpec((1, 1, 64, C), lambda f, i: (f, CHUNK - 1, 0, 0)),
            pl.BlockSpec((1, 1, 64, C), lambda f, i: (f, CHUNK, 0, 0)),
        ]
        + [VMEM] * 5,
        out_specs=[pl.BlockSpec((1, CHUNK, 4, 16, C), lambda f, i: (f, i, 0, 0, 0)), VMEM],
        out_shape=[
            pltpu.HBM((2, 128, 4, 16, C), BF),
            pltpu.VMEM((64, 32, C), BF),
        ],
        scratch_shapes=[
            pltpu.VMEM((CHUNK + 2, 80, C), F32),
            pltpu.VMEM((CHUNK + 2, 16, 6 * C), BF),
            pltpu.VMEM((3 * 512, 2 * C), BF),
            pltpu.VMEM((32, 32, C), F32),
        ],
        compiler_params=params(),
        cost_estimate=pl.CostEstimate(
            flops=2 * 16384 * 9 * C * C, bytes_accessed=9 * 2**20, transcendentals=2 * 16384 * C
        ),
        name="conv_block",
    )(far, far, far, *near(top, bottom, left, right, weight))


def embed_kernel(received, own, other, out, rows, values):
    core = lax.axis_index("core")
    for r in range(8):
        for xh in range(2):
            for y in range(4):
                at = pl.ds(((r * 2 + xh) * 4 + y) * 32, 32)
                rows[at, :] = received[in_same(r, xh, y)].astype(F32)
    for j in range(8):
        values[:, pl.ds(j * C, C)] = rows[pl.ds(j, 256, stride=8), :].astype(BF)
    for which, weight in enumerate((own, other)):
        wide = jnp.concatenate([weight[y, pl.ds(0, 1024)] for y in range(4)], axis=1)
        result = jnp.dot(values[...], wide, preferred_element_type=F32).astype(BF)
        feature = core if which == 0 else 1 - core
        for r in range(8):
            for y in range(4):
                out[in_rowy(r, y), feature] = result[r * 32 : r * 32 + 32, y * C : y * C + C]


def embed(received, own, other):
    return pl.pallas_call(
        embed_kernel,
        out_shape=pltpu.VMEM((32, 2, 32, C), BF),
        scratch_shapes=[
            pltpu.VMEM((2048 + 8, C), F32),
            pltpu.VMEM((256, 1024), BF),
        ],
        compiler_params=params(),
        name="embed",
    )(*near(received, own, other))


def sum_kernel(copies, terms, *rest):
    out, total_out = rest[-2:]
    total = terms[0].astype(F32)
    for i in range(1, terms.shape[0]):
        total = total + terms[i].astype(F32)
    if len(rest) == 3:
        total = rest[0][...].astype(F32) + total
    total = total.astype(BF)
    total_out[...] = total
    for i in range(copies):
        out[i] = total


def sum_and_copy(copies, terms, *base):
    return pl.pallas_call(
        functools.partial(sum_kernel, copies),
        out_shape=[pltpu.VMEM((copies, 2, 32, C), BF), pltpu.VMEM((2, 32, C), BF)],
        compiler_params=params(),
        name="sum_and_copy",
    )(*near(terms, *base))


def qkv_kernel(embedded, weight, queries, pairs):
    normed = []
    for core in range(2):
        blocks = [
            embedded[core * 8 + pair % 4 * 2 + pair // 4, feature].astype(F32)
            for pair in range(8)
            for feature in range(2)
        ]
        square = sum(block * block for block in blocks)
        square = jnp.sum(square, axis=-1, keepdims=True)
        scale = lax.rsqrt(square * (1.0 / 2048.0) + EPS)
        normed.append(jnp.concatenate([(block * scale).astype(BF) for block in blocks], axis=1))
    normed = jnp.concatenate(normed, axis=0)
    queries[...] = jnp.dot(normed, weight[0], preferred_element_type=F32).astype(BF)
    for part in range(2):
        result = jnp.dot(normed, weight[1 + part], preferred_element_type=F32).astype(BF)
        for r in range(8):
            pairs[r, part] = result


def project_qkv(embedded, weight):
    return pl.pallas_call(
        qkv_kernel,
        out_shape=[pltpu.VMEM((64, C), BF), pltpu.VMEM((8, 2, 64, C), BF)],
        compiler_params=params(),
        name="qkv",
    )(*near(embedded, weight))


def attend_kernel(queries, pairs, weight, out):
    keys = pairs[:, 0].reshape(512, C)
    values = pairs[:, 1].reshape(512, C)
    scores = lax.dot_general(
        queries[...], keys, (((1,), (1,)), ((), ())), preferred_element_type=F32
    ) * C ** (-0.5)
    scores = jnp.exp(scores - jnp.max(scores, axis=-1, keepdims=True))
    weights = (scores / jnp.sum(scores, axis=-1, keepdims=True)).astype(BF)
    attended = jnp.dot(weights, values, preferred_element_type=F32).astype(BF)
    projected = jnp.dot(attended, weight[...], preferred_element_type=F32).astype(BF)
    for pair in range(8):
        for which in range(2):
            target = which * 8 + pair % 4 * 2 + pair // 4
            for feature in range(2):
                at = (pair * 2 + feature) * C
                out[target, feature] = projected[which * 32 : which * 32 + 32, at : at + C]


def attend(queries, pairs, weight):
    return pl.pallas_call(
        attend_kernel,
        out_shape=pltpu.VMEM((16, 2, 32, C), BF),
        compiler_params=params(),
        name="attend",
    )(*near(queries, pairs, weight))


def unembed_kernel(mixed, own, other, out, values, rows):
    core = lax.axis_index("core")
    for which in range(2):
        feature = core if which == 0 else 1 - core
        for y in range(4):
            for r in range(8):
                at = pl.ds((which * 4 + y) * C, C)
                values[pl.ds(r * 32, 32), at] = mixed[in_rowy(r, y), feature]
    for pair in range(4):
        at = pl.ds(1024 + pair * 2 * C, 2 * C)
        wide = [weight[y, at] for weight in (own, other) for y in range(4)]
        result = lax.dot_general(
            values[...],
            jnp.concatenate(wide, axis=1),
            (((1,), (1,)), ((), ())),
            preferred_element_type=F32,
        )
        for j in range(2):
            column = result[:, j * C : j * C + C]
            rows[pl.ds(2 * pair + j, 256, stride=8), :] = column
    for r in range(8):
        for xh in range(2):
            for y in range(4):
                at = pl.ds(((r * 2 + xh) * 4 + y) * 32, 32)
                out[in_same(r, xh, y)] = rows[at, :].astype(BF)


def unembed(mixed, own, other):
    return pl.pallas_call(
        unembed_kernel,
        out_shape=pltpu.VMEM((64, 32, C), BF),
        scratch_shapes=[
            pltpu.VMEM((256, 1024), BF),
            pltpu.VMEM((2048 + 8, C), F32),
        ],
        compiler_params=params(),
        name="unembed",
    )(*near(mixed, own, other))


def finish_kernel(features, received, out, patch, spread):
    frame, step = pl.program_id(0), pl.program_id(1)

    @pl.when((frame == 0) & (step == 0))
    def _():
        for r in range(8):
            for y in range(4):
                first, second = (received[in_same(r, xh, y)].astype(F32) for xh in range(2))
                total = first + second
                patch[r * 4 + y] = total.astype(BF).astype(F32)

    for q in range(SPREAD // 4):
        token = frame * 2 + q // 16
        at = pl.ds(pl.multiple_of(token * 8, 8), 8)
        piece = q % 16 * 2
        small = jnp.concatenate([patch[piece, at, :], patch[piece + 1, at, :]], axis=0)
        for row in range(4):
            for m in range(4):
                value = features[frame, step * SPREAD + q * 4 + row, m].astype(F32) + small
                spread[q * 4 + row, pl.ds(m, 16, stride=4), :] = value
    out[0] = spread[:, pl.ds(0, 64), :].astype(BF)


def finish(features, received):
    return pl.pallas_call(
        finish_kernel,
        grid=(2, 128 // SPREAD),
        in_specs=[VMEM, VMEM],
        out_specs=pl.BlockSpec((1, SPREAD, 64, C), lambda f, i: (f, i, 0, 0)),
        out_shape=jax.ShapeDtypeStruct((2, 128, 64, C), BF),
        scratch_shapes=[
            pltpu.VMEM((32, 32, C), F32),
            pltpu.VMEM((SPREAD, 64 + 8, C), F32),
        ],
        compiler_params=params(),
        name="finish",
    )(*near(features, received))


def exchange(array, axes):
    return lax.all_to_all(array, axes, 0, 0, tiled=True)


def from_neighbours(low, high, axes, count):
    forward = [(i, i + 1) for i in range(count - 1)]
    backward = [(i + 1, i) for i in range(count - 1)]
    return lax.ppermute(low, axes, forward), lax.ppermute(high, axes, backward)


def on_device(frames, conv_weight, embed_weight, unembed_weight, qkv_weight, out_weight):
    left, right = from_neighbours(frames[:, :, 63], frames[:, :, 0], COL, 16)
    maps = [weight.reshape(4, 1024, C) for weight in (embed_weight, unembed_weight)]
    both = pack(*maps)
    left, right, both = lax.optimization_barrier((left, right, both))
    rows = [
        jnp.pad(
            jnp.concatenate([frames[:, y], left[:, y : y + 1], right[:, y : y + 1]], axis=1),
            ((0, 0), (0, 14), (0, 0)),
        )
        for y in (127, 0)
    ]
    top, bottom = from_neighbours(rows[0], rows[1], ROW, 8)
    own = exchange(both, "y")
    features, patches = convolve(frames, top, bottom, left, right, conv_weight)
    own, patches = lax.optimization_barrier((own, patches))
    other = lax.ppermute(own, "core", SWAP)
    partial = embed(exchange(patches, SAME), own, other)
    copies, embedded = sum_and_copy(16, exchange(partial, ROWY))
    queries, pairs = project_qkv(exchange(copies, ACROSS), qkv_weight)
    projected = attend(queries, exchange(pairs, ROW), out_weight)
    copies, _ = sum_and_copy(32, exchange(projected, ACROSS), embedded)
    patch_values = unembed(exchange(copies, ROWY), own, other)
    return finish(features, exchange(patch_values, SAME))


def solution(mesh):
    fine = jax.sharding.Mesh(mesh.devices.reshape(4, 2, 2, 4, 2), EVERY)
    placed = (
        P(None, ROW, COL, None),
        P(),
        P(ROW, COL),
        P(ROW, COL),
        P(None, None, COL),
        P(COL, None),
    )
    return jax.shard_map(
        on_device,
        mesh=fine,
        in_specs=placed,
        out_specs=P(None, ROW, COL, None),
        check_vma=False,
    )
```

```python
import functools

import jax
import jax.numpy as jnp
from jax import lax
from jax.experimental import pallas as pl
from jax.experimental.pallas import tpu as pltpu
from jax.sharding import PartitionSpec as P

C = 128
BF = jnp.bfloat16
F32 = jnp.float32
EPS = 1e-06
ROW = ("z", "xl")
COL = ("xh", "y", "core")
ACROSS = ("core", "y", "xh")
GATHER = ("xl", "z", "y")
ROWY = ("xl", "y", "z")
PATCHES = ("xh", "y", "z", "xl")
SAME = ("y", "xh", "xl", "z")
EVERY = ROW + COL
SWAP = [(0, 1), (1, 0)]
CHUNK = 64
SPREAD = 128
SUB = 8
LEFT = 8


def params(mib=12):
    return pltpu.CompilerParams(vmem_limit_bytes=mib * 2**20)


def in_rowy(r, y):
    return ((r % 2) * 4 + y) * 4 + r // 2


def in_same(r, xh, y):
    return ((y * 2 + xh) * 2 + r % 2) * 4 + r // 2


def in_patches(r, xh, y):
    return (xh * 4 + y) * 8 + r


def in_gather(r, y):
    return (r % 2 * 4 + r // 2) * 4 + y


def near(*arrays):
    return [pltpu.with_memory_space_constraint(array, pltpu.VMEM) for array in arrays]


VMEM = pl.BlockSpec(memory_space=pltpu.VMEM)


def pack_kernel(first, second, both, held, arrived, left):
    pieces = [(i, y, part) for i, part in enumerate((first, second)) for y in range(4)]
    loads = [
        pltpu.make_async_copy(part.at[y], held.at[i, y], arrived.at[i, y])
        for i, y, part in pieces
    ]
    stores = [
        pltpu.make_async_copy(held.at[i, y], both.at[y, pl.ds(1024 * i, 1024)], left.at[i, y])
        for i, y, _ in pieces
    ]
    for copy in loads:
        copy.start()
    for load, store in zip(loads, stores):
        load.wait()
        store.start()
    for copy in stores:
        copy.wait()


def pack(first, second):
    hbm = pl.BlockSpec(memory_space=pltpu.HBM)
    return pl.pallas_call(
        pack_kernel,
        in_specs=[hbm] * 2,
        out_specs=hbm,
        out_shape=pltpu.HBM((4, 2048, C), BF),
        scratch_shapes=[
            pltpu.VMEM((2, 4, 1024, C), BF),
            pltpu.SemaphoreType.DMA((2, 4)),
            pltpu.SemaphoreType.DMA((2, 4)),
        ],
        compiler_params=params(),
        name="pack",
    )(*(pltpu.with_memory_space_constraint(a, pltpu.HBM) for a in (first, second)))


def conv_kernel(
    main, above, below, top, bottom, left, right, weight, features, send, padded, taps, kernel, pooled
):
    frame, step = pl.program_id(0), pl.program_id(1)

    @pl.when((frame == 0) & (step == 0))
    def _():
        for a in range(3):
            for k in range(4):
                for o in range(2):
                    b = k - o
                    block = weight[a, b] if 0 <= b <= 2 else jnp.zeros((C, C), BF)
                    kernel[pl.ds(a * 512 + k * C, C), pl.ds(o * C, C)] = block

    cols = pl.ds(LEFT, 64)
    start = step * CHUNK
    padded[pl.ds(1, CHUNK), cols, :] = main[0].astype(F32)
    rows = pl.ds(pl.multiple_of(start, CHUNK), CHUNK)
    padded[pl.ds(1, CHUNK), LEFT - 1, :] = left[frame, rows, :].astype(F32)
    padded[pl.ds(1, CHUNK), LEFT + 64, :] = right[frame, rows, :].astype(F32)
    for border, outside, inside, row, at in (
        (step == 0, top, above, CHUNK - 1, 0),
        (step == 1, bottom, below, CHUNK, CHUNK + 1),
    ):

        @pl.when(border)
        def _(outside=outside, at=at):
            padded[at, cols, :] = outside[frame, pl.ds(0, 64)].astype(F32)
            corners = outside[frame, pl.ds(64, 16)].astype(F32)
            padded[at, pl.ds(LEFT - 1, 1), :] = corners[:1]
            padded[at, pl.ds(LEFT + 64, 1), :] = corners[1:2]

        @pl.when(jnp.logical_not(border))
        def _(inside=inside, row=row, at=at):
            padded[at, cols, :] = inside[0, 0].astype(F32)
            near_row = pl.ds(row // 16 * 16, 16)
            for side, col in ((left, LEFT - 1), (right, LEFT + 64)):
                value = side[frame, near_row, :].astype(F32)
                padded[at, pl.ds(col, 1), :] = value[row % 16 : row % 16 + 1]

    for k in range(6):
        taps[:, :, pl.ds(k * C, C)] = padded[:, pl.ds(LEFT - 1 + k, 16, stride=4), :].astype(BF)

    for sub in range(CHUNK // SUB):
        total = jnp.zeros((SUB // 4, 16, C), F32)
        for pair in range(2):
            lhs = jnp.concatenate(
                [
                    taps[pl.ds(sub * SUB + a, SUB), :, pl.ds(pair * 256, 512)].reshape(SUB * 16, 512)
                    for a in range(3)
                ],
                axis=1,
            )
            result = jnp.dot(lhs, kernel[...], preferred_element_type=F32)
            for o in range(2):
                m = pair * 2 + o
                v = result[:, o * C : (o + 1) * C]
                mean = jnp.mean(v * v, axis=-1, keepdims=True)
                h = v * (0.5 * lax.rsqrt(mean + EPS))
                x = taps[pl.ds(sub * SUB + 1, SUB), :, pl.ds((m + 1) * C, C)].reshape(SUB * 16, C)
                f = x.astype(F32) + (h + h * jnp.tanh(h))
                f = f.reshape(SUB, 16, C)
                features[0, pl.ds(sub * SUB, SUB), m] = f.astype(BF)
                total = total + f.reshape(SUB // 4, 4, 16, C).sum(axis=1)
        mean = total * (1.0 / 16.0)
        for g in range(SUB // 4):
            q = sub * (SUB // 4) + g
            token = frame * 2 + step
            for half in range(2):
                piece = q * 2 + half
                at = pl.ds(pl.multiple_of(token * 8, 8), 8)
                pooled[piece, at, :] = mean[g, half * 8 : half * 8 + 8]

    @pl.when((frame == 1) & (step == 1))
    def _():
        for r in range(8):
            for y in range(4):
                block = pooled[r * 4 + y].astype(BF)
                for xh in range(2):
                    send[in_patches(r, xh, y)] = block


def convolve(frames, top, bottom, left, right, weight):
    steps = 128 // CHUNK
    far = pltpu.with_memory_space_constraint(frames, pltpu.HBM)
    return pl.pallas_call(
        conv_kernel,
        grid=(2, steps),
        in_specs=[
            pl.BlockSpec((1, CHUNK, 64, C), lambda f, i: (f, i, 0, 0)),
            pl.BlockSpec((1, 1, 64, C), lambda f, i: (f, CHUNK - 1, 0, 0)),
            pl.BlockSpec((1, 1, 64, C), lambda f, i: (f, CHUNK, 0, 0)),
        ]
        + [VMEM] * 5,
        out_specs=[pl.BlockSpec((1, CHUNK, 4, 16, C), lambda f, i: (f, i, 0, 0, 0)), VMEM],
        out_shape=[
            pltpu.HBM((2, 128, 4, 16, C), BF),
            pltpu.VMEM((64, 32, C), BF),
        ],
        scratch_shapes=[
            pltpu.VMEM((CHUNK + 2, 80, C), F32),
            pltpu.VMEM((CHUNK + 2, 16, 6 * C), BF),
            pltpu.VMEM((3 * 512, 2 * C), BF),
            pltpu.VMEM((32, 32, C), F32),
        ],
        compiler_params=params(),
        cost_estimate=pl.CostEstimate(
            flops=2 * 16384 * 9 * C * C, bytes_accessed=9 * 2**20, transcendentals=2 * 16384 * C
        ),
        name="conv_block",
    )(far, far, far, *near(top, bottom, left, right, weight))


def embed_kernel(received, own, other, out, rows, values):
    core = lax.axis_index("core")
    for r in range(8):
        for xh in range(2):
            for y in range(4):
                at = pl.ds(((r * 2 + xh) * 4 + y) * 32, 32)
                rows[at, :] = received[in_patches(r, xh, y)].astype(F32)
    for j in range(8):
        values[:, pl.ds(j * C, C)] = rows[pl.ds(j, 256, stride=8), :].astype(BF)
    for which, weight in enumerate((own, other)):
        wide = jnp.concatenate([weight[y, pl.ds(0, 1024)] for y in range(4)], axis=1)
        result = jnp.dot(values[...], wide, preferred_element_type=F32).astype(BF)
        feature = core if which == 0 else 1 - core
        for r in range(8):
            for y in range(4):
                out[in_rowy(r, y), feature] = result[r * 32 : r * 32 + 32, y * C : y * C + C]


def embed(received, own, other):
    return pl.pallas_call(
        embed_kernel,
        out_shape=pltpu.VMEM((32, 2, 32, C), BF),
        scratch_shapes=[
            pltpu.VMEM((2048 + 8, C), F32),
            pltpu.VMEM((256, 1024), BF),
        ],
        compiler_params=params(),
        name="embed",
    )(*near(received, own, other))


def sum_kernel(copies, terms, *rest):
    out, total_out = rest[-2:]
    total = terms[0].astype(F32)
    for i in range(1, terms.shape[0]):
        total = total + terms[i].astype(F32)
    if len(rest) == 3:
        total = rest[0][...].astype(F32) + total
    total = total.astype(BF)
    total_out[...] = total
    for i in range(copies):
        out[i] = total


def sum_and_copy(copies, terms, *base):
    return pl.pallas_call(
        functools.partial(sum_kernel, copies),
        out_shape=[pltpu.VMEM((copies, 2, 32, C), BF), pltpu.VMEM((2, 32, C), BF)],
        compiler_params=params(),
        name="sum_and_copy",
    )(*near(terms, *base))


def qkv_kernel(embedded, weight, queries, pairs):
    normed = []
    for core in range(2):
        blocks = [
            embedded[core * 8 + pair % 4 * 2 + pair // 4, feature].astype(F32)
            for pair in range(8)
            for feature in range(2)
        ]
        square = sum(block * block for block in blocks)
        square = jnp.sum(square, axis=-1, keepdims=True)
        scale = lax.rsqrt(square * (1.0 / 2048.0) + EPS)
        normed.append(jnp.concatenate([(block * scale).astype(BF) for block in blocks], axis=1))
    normed = jnp.concatenate(normed, axis=0)
    queries[...] = jnp.dot(normed, weight[0], preferred_element_type=F32).astype(BF)
    for part in range(2):
        result = jnp.dot(normed, weight[1 + part], preferred_element_type=F32).astype(BF)
        for r in range(8):
            pairs[r, part] = result


def project_qkv(embedded, weight):
    return pl.pallas_call(
        qkv_kernel,
        out_shape=[pltpu.VMEM((64, C), BF), pltpu.VMEM((8, 2, 64, C), BF)],
        compiler_params=params(),
        name="qkv",
    )(*near(embedded, weight))


def attend_kernel(queries, pairs, weight, out):
    keys = pairs[:, 0].reshape(512, C)
    values = pairs[:, 1].reshape(512, C)
    scores = lax.dot_general(
        queries[...], keys, (((1,), (1,)), ((), ())), preferred_element_type=F32
    ) * C ** (-0.5)
    scores = jnp.exp(scores - jnp.max(scores, axis=-1, keepdims=True))
    weights = (scores / jnp.sum(scores, axis=-1, keepdims=True)).astype(BF)
    attended = jnp.dot(weights, values, preferred_element_type=F32).astype(BF)
    projected = jnp.dot(attended, weight[...], preferred_element_type=F32).astype(BF)
    for pair in range(8):
        for which in range(2):
            target = which * 8 + pair % 4 * 2 + pair // 4
            for feature in range(2):
                at = (pair * 2 + feature) * C
                out[target, feature] = projected[which * 32 : which * 32 + 32, at : at + C]


def attend(queries, pairs, weight):
    return pl.pallas_call(
        attend_kernel,
        out_shape=pltpu.VMEM((16, 2, 32, C), BF),
        compiler_params=params(),
        name="attend",
    )(*near(queries, pairs, weight))


def unembed_kernel(mixed, own, other, out, values, rows):
    core = lax.axis_index("core")
    for which in range(2):
        feature = core if which == 0 else 1 - core
        for y in range(4):
            for r in range(8):
                at = pl.ds((which * 4 + y) * C, C)
                values[pl.ds(r * 32, 32), at] = mixed[in_gather(r, y), feature]
    for pair in range(4):
        at = pl.ds(1024 + pair * 2 * C, 2 * C)
        wide = [weight[y, at] for weight in (own, other) for y in range(4)]
        result = lax.dot_general(
            values[...],
            jnp.concatenate(wide, axis=1),
            (((1,), (1,)), ((), ())),
            preferred_element_type=F32,
        )
        for j in range(2):
            column = result[:, j * C : j * C + C]
            rows[pl.ds(2 * pair + j, 256, stride=8), :] = column
    for r in range(8):
        for xh in range(2):
            for y in range(4):
                at = pl.ds(((r * 2 + xh) * 4 + y) * 32, 32)
                out[in_same(r, xh, y)] = rows[at, :].astype(BF)


def unembed(mixed, own, other):
    return pl.pallas_call(
        unembed_kernel,
        out_shape=pltpu.VMEM((64, 32, C), BF),
        scratch_shapes=[
            pltpu.VMEM((256, 1024), BF),
            pltpu.VMEM((2048 + 8, C), F32),
        ],
        compiler_params=params(),
        name="unembed",
    )(*near(mixed, own, other))


def finish_kernel(features, received, out, patch, spread):
    frame, step = pl.program_id(0), pl.program_id(1)

    @pl.when((frame == 0) & (step == 0))
    def _():
        for r in range(8):
            for y in range(4):
                first, second = (received[in_same(r, xh, y)].astype(F32) for xh in range(2))
                total = first + second
                patch[r * 4 + y] = total.astype(BF).astype(F32)

    for q in range(SPREAD // 4):
        token = frame * 2 + q // 16
        at = pl.ds(pl.multiple_of(token * 8, 8), 8)
        piece = q % 16 * 2
        small = jnp.concatenate([patch[piece, at, :], patch[piece + 1, at, :]], axis=0)
        for row in range(4):
            for m in range(4):
                value = features[frame, step * SPREAD + q * 4 + row, m].astype(F32) + small
                spread[q * 4 + row, pl.ds(m, 16, stride=4), :] = value
    out[0] = spread[:, pl.ds(0, 64), :].astype(BF)


def finish(features, received):
    return pl.pallas_call(
        finish_kernel,
        grid=(2, 128 // SPREAD),
        in_specs=[VMEM, VMEM],
        out_specs=pl.BlockSpec((1, SPREAD, 64, C), lambda f, i: (f, i, 0, 0)),
        out_shape=jax.ShapeDtypeStruct((2, 128, 64, C), BF),
        scratch_shapes=[
            pltpu.VMEM((32, 32, C), F32),
            pltpu.VMEM((SPREAD, 64 + 8, C), F32),
        ],
        compiler_params=params(),
        name="finish",
    )(*near(features, received))


def exchange(array, axes):
    return lax.all_to_all(array, axes, 0, 0, tiled=True)


def from_neighbours(low, high, axes, count):
    forward = [(i, i + 1) for i in range(count - 1)]
    backward = [(i + 1, i) for i in range(count - 1)]
    return lax.ppermute(low, axes, forward), lax.ppermute(high, axes, backward)


def on_device(frames, conv_weight, embed_weight, unembed_weight, qkv_weight, out_weight):
    left, right = from_neighbours(frames[:, :, 63], frames[:, :, 0], COL, 16)
    maps = [weight.reshape(4, 1024, C) for weight in (embed_weight, unembed_weight)]
    both = pack(*maps)
    left, right, both = lax.optimization_barrier((left, right, both))
    rows = [
        jnp.pad(
            jnp.concatenate([frames[:, y], left[:, y : y + 1], right[:, y : y + 1]], axis=1),
            ((0, 0), (0, 14), (0, 0)),
        )
        for y in (127, 0)
    ]
    top, bottom = from_neighbours(rows[0], rows[1], ROW, 8)
    own = exchange(both, "y")
    features, patches = convolve(frames, top, bottom, left, right, conv_weight)
    own, patches = lax.optimization_barrier((own, patches))
    other = lax.ppermute(own, "core", SWAP)
    partial = embed(exchange(patches, PATCHES), own, other)
    copies, embedded = sum_and_copy(16, exchange(partial, ROWY))
    queries, pairs = project_qkv(exchange(copies, ACROSS), qkv_weight)
    projected = attend(queries, exchange(pairs, ROW), out_weight)
    copies, _ = sum_and_copy(32, exchange(projected, ACROSS), embedded)
    patch_values = unembed(exchange(copies, GATHER), own, other)
    return finish(features, exchange(patch_values, SAME))


def solution(mesh):
    fine = jax.sharding.Mesh(mesh.devices.reshape(4, 2, 2, 4, 2), EVERY)
    placed = (
        P(None, ROW, COL, None),
        P(),
        P(ROW, COL),
        P(ROW, COL),
        P(None, None, COL),
        P(COL, None),
    )
    return jax.shard_map(
        on_device,
        mesh=fine,
        in_specs=placed,
        out_specs=P(None, ROW, COL, None),
        check_vma=False,
    )
```

```python
import functools

import jax
import jax.numpy as jnp
from jax import lax
from jax.experimental import pallas as pl
from jax.experimental.pallas import tpu as pltpu
from jax.sharding import PartitionSpec as P

C = 128
BF = jnp.bfloat16
F32 = jnp.float32
EPS = 1e-06
ROW = ("z", "xl")
COL = ("xh", "y", "core")
ACROSS = ("core", "y", "xh")
GATHER = ("xl", "z", "y")
ROWY = ("xl", "y", "z")
PATCHES = ("xh", "y", "z", "xl")
SAME = ("y", "xh", "xl", "z")
EVERY = ROW + COL
SWAP = [(0, 1), (1, 0)]
CHUNK = 64
SPREAD = 128
SUB = 8
LEFT = 8


def params(mib=12):
    return pltpu.CompilerParams(vmem_limit_bytes=mib * 2**20)


def in_rowy(r, y):
    return ((r % 2) * 4 + y) * 4 + r // 2


def in_same(r, xh, y):
    return ((y * 2 + xh) * 2 + r % 2) * 4 + r // 2


def in_patches(r, xh, y):
    return (xh * 4 + y) * 8 + r


def in_gather(r, y):
    return (r % 2 * 4 + r // 2) * 4 + y


def near(*arrays):
    return [pltpu.with_memory_space_constraint(array, pltpu.VMEM) for array in arrays]


VMEM = pl.BlockSpec(memory_space=pltpu.VMEM)


def pack_kernel(first, second, both, held, arrived, left):
    pieces = [(i, y, part) for i, part in enumerate((first, second)) for y in range(4)]
    loads = [
        pltpu.make_async_copy(part.at[y], held.at[i, y], arrived.at[i, y])
        for i, y, part in pieces
    ]
    stores = [
        pltpu.make_async_copy(held.at[i, y], both.at[y, pl.ds(1024 * i, 1024)], left.at[i, y])
        for i, y, _ in pieces
    ]
    for copy in loads:
        copy.start()
    for load, store in zip(loads, stores):
        load.wait()
        store.start()
    for copy in stores:
        copy.wait()


def pack(first, second):
    hbm = pl.BlockSpec(memory_space=pltpu.HBM)
    return pl.pallas_call(
        pack_kernel,
        in_specs=[hbm] * 2,
        out_specs=hbm,
        out_shape=pltpu.HBM((4, 2048, C), BF),
        scratch_shapes=[
            pltpu.VMEM((2, 4, 1024, C), BF),
            pltpu.SemaphoreType.DMA((2, 4)),
            pltpu.SemaphoreType.DMA((2, 4)),
        ],
        compiler_params=params(),
        name="pack",
    )(*(pltpu.with_memory_space_constraint(a, pltpu.HBM) for a in (first, second)))


def conv_kernel(
    main, above, below, top, bottom, left, right, weight, features, send, padded, taps, kernel, pooled
):
    frame, step = pl.program_id(0), pl.program_id(1)

    @pl.when((frame == 0) & (step == 0))
    def _():
        for a in range(3):
            for k in range(4):
                for o in range(2):
                    b = k - o
                    block = weight[a, b] if 0 <= b <= 2 else jnp.zeros((C, C), BF)
                    kernel[pl.ds(a * 512 + k * C, C), pl.ds(o * C, C)] = block

    cols = pl.ds(LEFT, 64)
    start = step * CHUNK
    padded[pl.ds(1, CHUNK), cols, :] = main[0].astype(F32)
    rows = pl.ds(pl.multiple_of(start, CHUNK), CHUNK)
    padded[pl.ds(1, CHUNK), LEFT - 1, :] = left[frame, rows, :].astype(F32)
    padded[pl.ds(1, CHUNK), LEFT + 64, :] = right[frame, rows, :].astype(F32)
    for border, outside, inside, row, at in (
        (step == 0, top, above, CHUNK - 1, 0),
        (step == 1, bottom, below, CHUNK, CHUNK + 1),
    ):

        @pl.when(border)
        def _(outside=outside, at=at):
            padded[at, cols, :] = outside[frame, pl.ds(0, 64)].astype(F32)
            corners = outside[frame, pl.ds(64, 16)].astype(F32)
            padded[at, pl.ds(LEFT - 1, 1), :] = corners[:1]
            padded[at, pl.ds(LEFT + 64, 1), :] = corners[1:2]

        @pl.when(jnp.logical_not(border))
        def _(inside=inside, row=row, at=at):
            padded[at, cols, :] = inside[0, 0].astype(F32)
            near_row = pl.ds(row // 16 * 16, 16)
            for side, col in ((left, LEFT - 1), (right, LEFT + 64)):
                value = side[frame, near_row, :].astype(F32)
                padded[at, pl.ds(col, 1), :] = value[row % 16 : row % 16 + 1]

    for k in range(6):
        taps[:, :, pl.ds(k * C, C)] = padded[:, pl.ds(LEFT - 1 + k, 16, stride=4), :].astype(BF)

    for sub in range(CHUNK // SUB):
        total = jnp.zeros((SUB // 4, 16, C), F32)
        for pair in range(2):
            lhs = jnp.concatenate(
                [
                    taps[pl.ds(sub * SUB + a, SUB), :, pl.ds(pair * 256, 512)].reshape(SUB * 16, 512)
                    for a in range(3)
                ],
                axis=1,
            )
            result = jnp.dot(lhs, kernel[...], preferred_element_type=F32)
            for o in range(2):
                m = pair * 2 + o
                v = result[:, o * C : (o + 1) * C]
                mean = jnp.mean(v * v, axis=-1, keepdims=True)
                h = v * (0.5 * lax.rsqrt(mean + EPS))
                x = taps[pl.ds(sub * SUB + 1, SUB), :, pl.ds((m + 1) * C, C)].reshape(SUB * 16, C)
                f = x.astype(F32) + (h + h * jnp.tanh(h))
                f = f.reshape(SUB, 16, C)
                features[0, pl.ds(sub * SUB, SUB), m] = f.astype(BF)
                total = total + f.reshape(SUB // 4, 4, 16, C).sum(axis=1)
        mean = total * (1.0 / 16.0)
        for g in range(SUB // 4):
            q = sub * (SUB // 4) + g
            token = frame * 2 + step
            for half in range(2):
                piece = q * 2 + half
                at = pl.ds(pl.multiple_of(token * 8, 8), 8)
                pooled[piece, at, :] = mean[g, half * 8 : half * 8 + 8]

    @pl.when((frame == 1) & (step == 1))
    def _():
        for r in range(8):
            for y in range(4):
                block = pooled[r * 4 + y].astype(BF)
                for xh in range(2):
                    send[in_patches(r, xh, y)] = block


def convolve(frames, top, bottom, left, right, weight):
    steps = 128 // CHUNK
    far = pltpu.with_memory_space_constraint(frames, pltpu.HBM)
    return pl.pallas_call(
        conv_kernel,
        grid=(2, steps),
        in_specs=[
            pl.BlockSpec((1, CHUNK, 64, C), lambda f, i: (f, i, 0, 0)),
            pl.BlockSpec((1, 1, 64, C), lambda f, i: (f, CHUNK - 1, 0, 0)),
            pl.BlockSpec((1, 1, 64, C), lambda f, i: (f, CHUNK, 0, 0)),
        ]
        + [VMEM] * 5,
        out_specs=[pl.BlockSpec((1, CHUNK, 4, 16, C), lambda f, i: (f, i, 0, 0, 0)), VMEM],
        out_shape=[
            pltpu.HBM((2, 128, 4, 16, C), BF),
            pltpu.VMEM((64, 32, C), BF),
        ],
        scratch_shapes=[
            pltpu.VMEM((CHUNK + 2, 80, C), F32),
            pltpu.VMEM((CHUNK + 2, 16, 6 * C), BF),
            pltpu.VMEM((3 * 512, 2 * C), BF),
            pltpu.VMEM((32, 32, C), F32),
        ],
        compiler_params=params(),
        cost_estimate=pl.CostEstimate(
            flops=2 * 16384 * 9 * C * C, bytes_accessed=9 * 2**20, transcendentals=2 * 16384 * C
        ),
        name="conv_block",
    )(far, far, far, *near(top, bottom, left, right, weight))


def embed_kernel(received, own, other, out, rows, values):
    core = lax.axis_index("core")
    for r in range(8):
        for xh in range(2):
            for y in range(4):
                at = pl.ds(((r * 2 + xh) * 4 + y) * 32, 32)
                rows[at, :] = received[in_patches(r, xh, y)].astype(F32)
    for j in range(8):
        values[:, pl.ds(j * C, C)] = rows[pl.ds(j, 256, stride=8), :].astype(BF)
    for which, weight in enumerate((own, other)):
        wide = jnp.concatenate([weight[y, pl.ds(0, 1024)] for y in range(4)], axis=1)
        result = jnp.dot(values[...], wide, preferred_element_type=F32).astype(BF)
        feature = core if which == 0 else 1 - core
        for r in range(8):
            for y in range(4):
                out[in_rowy(r, y), feature] = result[r * 32 : r * 32 + 32, y * C : y * C + C]


def embed(received, own, other):
    return pl.pallas_call(
        embed_kernel,
        out_shape=pltpu.VMEM((32, 2, 32, C), BF),
        scratch_shapes=[
            pltpu.VMEM((2048 + 8, C), F32),
            pltpu.VMEM((256, 1024), BF),
        ],
        compiler_params=params(),
        name="embed",
    )(*near(received, own, other))


def sum_kernel(copies, terms, out, total_out):
    total = terms[0].astype(F32)
    for i in range(1, terms.shape[0]):
        total = total + terms[i].astype(F32)
    total = total.astype(BF)
    total_out[...] = total
    for i in range(copies):
        out[i] = total


def sum_and_copy(copies, terms):
    return pl.pallas_call(
        functools.partial(sum_kernel, copies),
        out_shape=[pltpu.VMEM((copies, 2, 32, C), BF), pltpu.VMEM((2, 32, C), BF)],
        compiler_params=params(),
        name="sum_and_copy",
    )(*near(terms))


def mix_kernel(copies, terms, base, out):
    total = base[...].astype(F32)
    for i in range(terms.shape[0]):
        total = total + terms[i].astype(F32)
    total = total.astype(BF)
    for i in range(copies):
        out[i] = total


def mix_and_copy(copies, terms, base):
    return pl.pallas_call(
        functools.partial(mix_kernel, copies),
        out_shape=pltpu.VMEM((copies, 2, 32, C), BF),
        compiler_params=params(),
        name="mix_and_copy",
    )(*near(terms, base))


def qkv_kernel(embedded, weight, queries, pairs):
    normed = []
    for core in range(2):
        blocks = [
            embedded[core * 8 + pair % 4 * 2 + pair // 4, feature].astype(F32)
            for pair in range(8)
            for feature in range(2)
        ]
        square = sum(block * block for block in blocks)
        square = jnp.sum(square, axis=-1, keepdims=True)
        scale = lax.rsqrt(square * (1.0 / 2048.0) + EPS)
        normed.append(jnp.concatenate([(block * scale).astype(BF) for block in blocks], axis=1))
    normed = jnp.concatenate(normed, axis=0)
    queries[...] = jnp.dot(normed, weight[0], preferred_element_type=F32).astype(BF)
    for part in range(2):
        result = jnp.dot(normed, weight[1 + part], preferred_element_type=F32).astype(BF)
        for r in range(8):
            pairs[r, part] = result


def project_qkv(embedded, weight):
    return pl.pallas_call(
        qkv_kernel,
        out_shape=[pltpu.VMEM((64, C), BF), pltpu.VMEM((8, 2, 64, C), BF)],
        compiler_params=params(),
        name="qkv",
    )(*near(embedded, weight))


def attend_kernel(queries, pairs, weight, out):
    keys = pairs[:, 0].reshape(512, C)
    values = pairs[:, 1].reshape(512, C)
    scores = lax.dot_general(
        queries[...], keys, (((1,), (1,)), ((), ())), preferred_element_type=F32
    ) * C ** (-0.5)
    scores = jnp.exp(scores - jnp.max(scores, axis=-1, keepdims=True))
    weights = (scores / jnp.sum(scores, axis=-1, keepdims=True)).astype(BF)
    attended = jnp.dot(weights, values, preferred_element_type=F32).astype(BF)
    projected = jnp.dot(attended, weight[...], preferred_element_type=F32).astype(BF)
    for pair in range(8):
        for which in range(2):
            target = which * 8 + pair % 4 * 2 + pair // 4
            for feature in range(2):
                at = (pair * 2 + feature) * C
                out[target, feature] = projected[which * 32 : which * 32 + 32, at : at + C]


def attend(queries, pairs, weight):
    return pl.pallas_call(
        attend_kernel,
        out_shape=pltpu.VMEM((16, 2, 32, C), BF),
        compiler_params=params(),
        name="attend",
    )(*near(queries, pairs, weight))


def unembed_kernel(mixed, own, other, out, values, rows):
    core = lax.axis_index("core")
    for which in range(2):
        feature = core if which == 0 else 1 - core
        for y in range(4):
            for r in range(8):
                at = pl.ds((which * 4 + y) * C, C)
                values[pl.ds(r * 32, 32), at] = mixed[in_gather(r, y), feature]
    for pair in range(4):
        at = pl.ds(1024 + pair * 2 * C, 2 * C)
        wide = [weight[y, at] for weight in (own, other) for y in range(4)]
        result = lax.dot_general(
            values[...],
            jnp.concatenate(wide, axis=1),
            (((1,), (1,)), ((), ())),
            preferred_element_type=F32,
        )
        for j in range(2):
            column = result[:, j * C : j * C + C]
            rows[pl.ds(2 * pair + j, 256, stride=8), :] = column
    for r in range(8):
        for xh in range(2):
            for y in range(4):
                at = pl.ds(((r * 2 + xh) * 4 + y) * 32, 32)
                out[in_same(r, xh, y)] = rows[at, :].astype(BF)


def unembed(mixed, own, other):
    return pl.pallas_call(
        unembed_kernel,
        out_shape=pltpu.VMEM((64, 32, C), BF),
        scratch_shapes=[
            pltpu.VMEM((256, 1024), BF),
            pltpu.VMEM((2048 + 8, C), F32),
        ],
        compiler_params=params(),
        name="unembed",
    )(*near(mixed, own, other))


def finish_kernel(features, received, out, patch, spread):
    frame, step = pl.program_id(0), pl.program_id(1)

    @pl.when((frame == 0) & (step == 0))
    def _():
        for r in range(8):
            for y in range(4):
                first, second = (received[in_same(r, xh, y)].astype(F32) for xh in range(2))
                total = first + second
                patch[r * 4 + y] = total.astype(BF).astype(F32)

    for q in range(SPREAD // 4):
        token = frame * 2 + q // 16
        at = pl.ds(pl.multiple_of(token * 8, 8), 8)
        piece = q % 16 * 2
        small = jnp.concatenate([patch[piece, at, :], patch[piece + 1, at, :]], axis=0)
        for row in range(4):
            for m in range(4):
                value = features[frame, step * SPREAD + q * 4 + row, m].astype(F32) + small
                spread[q * 4 + row, pl.ds(m, 16, stride=4), :] = value
    out[0] = spread[:, pl.ds(0, 64), :].astype(BF)


def finish(features, received):
    return pl.pallas_call(
        finish_kernel,
        grid=(2, 128 // SPREAD),
        in_specs=[VMEM, VMEM],
        out_specs=pl.BlockSpec((1, SPREAD, 64, C), lambda f, i: (f, i, 0, 0)),
        out_shape=jax.ShapeDtypeStruct((2, 128, 64, C), BF),
        scratch_shapes=[
            pltpu.VMEM((32, 32, C), F32),
            pltpu.VMEM((SPREAD, 64 + 8, C), F32),
        ],
        compiler_params=params(),
        name="finish",
    )(*near(features, received))


def exchange(array, axes):
    return lax.all_to_all(array, axes, 0, 0, tiled=True)


def from_neighbours(low, high, axes, count):
    forward = [(i, i + 1) for i in range(count - 1)]
    backward = [(i + 1, i) for i in range(count - 1)]
    return lax.ppermute(low, axes, forward), lax.ppermute(high, axes, backward)


def on_device(frames, conv_weight, embed_weight, unembed_weight, qkv_weight, out_weight):
    left, right = from_neighbours(frames[:, :, 63], frames[:, :, 0], COL, 16)
    maps = [weight.reshape(4, 1024, C) for weight in (embed_weight, unembed_weight)]
    both = pack(*maps)
    left, right, both = lax.optimization_barrier((left, right, both))
    rows = [
        jnp.pad(
            jnp.concatenate([frames[:, y], left[:, y : y + 1], right[:, y : y + 1]], axis=1),
            ((0, 0), (0, 14), (0, 0)),
        )
        for y in (127, 0)
    ]
    top, bottom = from_neighbours(rows[0], rows[1], ROW, 8)
    own = exchange(both, "y")
    features, patches = convolve(frames, top, bottom, left, right, conv_weight)
    own, patches = lax.optimization_barrier((own, patches))
    other = lax.ppermute(own, "core", SWAP)
    partial = embed(exchange(patches, PATCHES), own, other)
    copies, embedded = sum_and_copy(16, exchange(partial, ROWY))
    queries, pairs = project_qkv(exchange(copies, ACROSS), qkv_weight)
    projected = attend(queries, exchange(pairs, ROW), out_weight)
    copies = mix_and_copy(32, exchange(projected, ACROSS), embedded)
    patch_values = unembed(exchange(copies, GATHER), own, other)
    return finish(features, exchange(patch_values, SAME))


def solution(mesh):
    fine = jax.sharding.Mesh(mesh.devices.reshape(4, 2, 2, 4, 2), EVERY)
    placed = (
        P(None, ROW, COL, None),
        P(),
        P(ROW, COL),
        P(ROW, COL),
        P(None, None, COL),
        P(COL, None),
    )
    return jax.shard_map(
        on_device,
        mesh=fine,
        in_specs=placed,
        out_specs=P(None, ROW, COL, None),
        check_vma=False,
    )
```
